32 devices in a mesh: hours: 2 (over y), pairs: 16 (over z, x, core).
Axes of the slice: x: 2, y: 2, z: 4, core: 2. Of those that a mesh axis runs over, the one named last changes fastest.
Arguments:
- spectra: bfloat16 [32, 2, 8, 256, 256], P(('hours', 'pairs')), parts along dimension 0, may hold values from -6 to 6
- pair_offset: int32 [32, 4], P(('hours', 'pairs')), parts along dimension 0, may hold values from 0 to 4
- lag_limit: int32 [32, 4], P(('hours', 'pairs')), parts along dimension 0, may hold values from 64 to 256
Outputs:
- correlations: bfloat16 [32, 4, 256, 512], P(('hours', 'pairs')), parts along dimension 0
The draws below stay inside these ranges and needn't reach their ends.
There are 2 independent parts, one for each index of `hours`. The reference program is written for one: setup_inputs(seed, part) draws one part's arguments, and reference() takes and returns one part's arrays. A program takes and returns all parts, laid end to end along the dimension named above; each array names one. Nothing has to cross between parts.
Inputs may be any that keep to these rules, and one draw needn't show every extreme that they name: `pair_offset`: slot k of block a pairs it with block a + value; 0 marks an empty slot; partners past the last block of the last fibre have zero spectra.
All inputs are finite; a program needn't handle non-finite values.
Results may differ from the reference program's by a relative error of at most 0.011.
Values may be sent and summed in bfloat16 or wider, within the bound.
No kernel may reach another device: no remote copies, remote signals or barrier semaphores. Data moves between devices by JAX's collectives and lax.ppermute only.
A program may use at most 128 MiB of HBM per device.

```python
import math
import jax
import jax.numpy as jnp
from jax import lax

CH = 256
F = 256
LAGS = 512
BAND_LO = 16
WIN = 8
SLOTS = 4
REACH = 4
BLOCKS = 16


def place_ends(result, rng, low, largest):
    shape = result.shape
    spot = [jax.random.randint(jax.random.fold_in(rng, axis), (), 0, shape[axis]) for axis in range(len(shape))]
    result = result.at[tuple(spot)].set(low)
    longest = shape.index(max(shape))
    spot[longest] = (spot[longest] + 1) % shape[longest]
    return result.at[tuple(spot)].set(largest)


def shard_levels(own_key, dims, cuts, smallest, largest):
    loudness, own = 1.0, jax.random.fold_in(own_key, 6)
    for dim, blocks in cuts:
        heights = jnp.exp(jax.random.uniform(jax.random.fold_in(own, dim), (blocks,), jnp.float32, smallest / len(cuts), largest / len(cuts)))
        loudness = loudness * jnp.repeat(heights, dims[dim] // blocks).reshape([-1 if axis == dim else 1 for axis in range(len(dims))])
    return loudness


def scatter_about(stream_key, dims, scale, most, pieces=(), held_as=jnp.bfloat16):
    entries = jax.random.normal(stream_key, dims, jnp.float32) * scale
    if len(pieces) > 0:
        entries = shard_levels(stream_key, dims, pieces, -0.22, 0.18) * entries
    return jnp.clip(entries, min=-most, max=most).astype(held_as)


def setup_inputs(seed: int = 0, part: int = 0) -> dict:
    seeds = jax.random.split(jax.random.key(seed), 4)
    part_keys = jax.random.split(jax.random.fold_in(seeds[3], part), 4)
    spectra = scatter_about(part_keys[0], (BLOCKS, 2, WIN, CH, F), 1.0, 6.0, ((0, 16),))
    pair_offset = place_ends(jax.random.randint(part_keys[1], (BLOCKS, SLOTS), 0, REACH + 1), jax.random.fold_in(part_keys[1], 1), 0, REACH).astype(jnp.int32)
    lag_limit = place_ends(jax.random.randint(part_keys[2], (BLOCKS, SLOTS), LAGS // 8, LAGS // 2 + 1), jax.random.fold_in(part_keys[2], 1), LAGS // 8, (LAGS // 2 + 1) - 1).astype(jnp.int32)
    return dict(spectra=spectra, pair_offset=pair_offset, lag_limit=lag_limit)


def whiten(block):
    values = block.astype(jnp.float32)
    power = lax.optimization_barrier(jnp.mean(values * values, axis=(-4, -1), keepdims=True))
    return (values * lax.rsqrt(power + 1e-06)).astype(jnp.bfloat16)

def phase_table(bins, lag_count):
    freq = jnp.arange(bins, dtype=jnp.int32) + BAND_LO
    lag_index = jnp.arange(lag_count, dtype=jnp.int32)
    phase = freq[:, None] * lag_index[None, :] % lag_count
    angle = 2.0 * math.pi / lag_count * phase.astype(jnp.float32)
    scale = 1.0 / math.sqrt(bins)
    return jnp.concatenate([jnp.cos(angle) * scale, -jnp.sin(angle) * scale], axis=0).astype(jnp.bfloat16)

def cross_lags(own_block, partners, offsets, limits, table):
    windows = own_block.shape[1]
    slot_count, channels = (partners.shape[0], partners.shape[3])
    lag_count = table.shape[1]
    first = own_block.astype(jnp.float32)
    second = partners.astype(jnp.float32)
    real_part = lax.optimization_barrier(jnp.sum(first[0] * second[:, 0] + first[1] * second[:, 1], axis=1)) / windows
    imag_part = lax.optimization_barrier(jnp.sum(first[0] * second[:, 1] - first[1] * second[:, 0], axis=1)) / windows
    spectrum = jnp.concatenate([real_part, imag_part], axis=-1).astype(jnp.bfloat16)
    lagged = jnp.dot(spectrum.reshape(slot_count * channels, -1), table, preferred_element_type=jnp.float32)
    lagged = lagged.reshape(slot_count, channels, lag_count)
    lag_index = jnp.arange(lag_count, dtype=jnp.int32)
    distance = jnp.minimum(lag_index, lag_count - lag_index)
    keep = (distance[None, :] < limits[:, None]) & (offsets[:, None] > 0)
    return jnp.where(keep[:, None, :], lagged, 0.0).astype(jnp.bfloat16)

def reference(spectra, pair_offset, lag_limit):
    whitened = whiten(spectra)
    padded = jnp.concatenate([whitened, jnp.zeros((REACH,) + whitened.shape[1:], jnp.bfloat16)], axis=0)
    table = phase_table(F, LAGS)
    indices = jnp.arange(BLOCKS, dtype=jnp.int32)

    def one_block(items):
        own_block, offsets, limits, index = items
        partners = jnp.take(padded, (index + offsets).astype(jnp.int32), axis=0)
        return cross_lags(own_block, partners, offsets, limits, table)
    return lax.map(one_block, (whitened, pair_offset, lag_limit, indices))
```

```python
import functools
import math

import jax
import jax.numpy as jnp
import numpy as np
from jax import lax
from jax.experimental import pallas as pl
from jax.experimental.pallas import tpu as pltpu
from jax.sharding import PartitionSpec as P

BAND_LO = 16
TILE = 16
LANES = 128
VMEM_LIMIT = 56 * 1024 * 1024


def whiten_kernel(position, mine_in, theirs_in, mine_out, theirs_out):
    windows, rows = mine_in.shape[2], mine_in.shape[3]
    for source, target in ((theirs_in, theirs_out), (mine_in, mine_out)):

        def one_window(w, _):
            for row in range(0, rows, TILE):
                block = pl.ds(row, TILE)
                values = source[0, :, w, block, :].astype(jnp.float32)
                power = jnp.sum(jnp.sum(values * values, axis=0), axis=-1, keepdims=True)
                power = power / (values.shape[0] * values.shape[-1])
                scaled = values * lax.rsqrt(power + 1e-06)
                target[0, :, w, block, :] = scaled.astype(jnp.bfloat16)
            return 0

        lax.fori_loop(0, windows, one_window, 0)


def whiten(position, spectra):
    parts, windows, channels, bins = spectra.shape[1:]
    rows = channels // 4
    block = (1, parts, windows, rows, bins)
    shape = jax.ShapeDtypeStruct((2, parts, windows, rows, bins), jnp.bfloat16)
    own = lambda k, position: (0, 0, 0, 2 * k + position[0], 0)
    other = lambda k, position: (0, 0, 0, 2 * k + 1 - position[0], 0)
    out = lambda k, position: (k, 0, 0, 0, 0)
    return pl.pallas_call(
        whiten_kernel,
        out_shape=(shape, shape),
        grid_spec=pltpu.PrefetchScalarGridSpec(
            num_scalar_prefetch=1,
            grid=(2,),
            in_specs=[pl.BlockSpec(block, own), pl.BlockSpec(block, other)],
            out_specs=[pl.BlockSpec(block, out), pl.BlockSpec(block, out)],
        ),
        compiler_params=pltpu.CompilerParams(vmem_limit_bytes=VMEM_LIMIT),
        cost_estimate=pl.CostEstimate(flops=5_000_000, bytes_accessed=4_000_000, transcendentals=0),
        name="whiten",
    )(position, spectra, spectra)


def products(first, second, stores, rows, bins, windows):
    def one_tile(step, _):
        row = pl.multiple_of(step * TILE, TILE)
        for lane in range(0, bins, LANES):
            reals = [[0.0] * len(second) for _ in first]
            imags = [[0.0] * len(second) for _ in first]
            for w in range(windows):
                a = [[f(part, w, row, lane) for part in range(2)] for f in first]
                b = [[f(part, w, row, lane) for part in range(2)] for f in second]
                for i, (ar, ai) in enumerate(a):
                    for j, (br, bi) in enumerate(b):
                        if not stores[i][j]:
                            continue
                        reals[i][j] = reals[i][j] + (ar * br + ai * bi)
                        imags[i][j] = imags[i][j] + (ar * bi - ai * br)
            for i in range(len(first)):
                for j in range(len(second)):
                    for ref, spot in stores[i][j]:
                        scale = 1.0 / windows
                        ref[spot, pl.ds(row, TILE), pl.ds(lane, LANES)] = (
                            reals[i][j] * scale
                        ).astype(jnp.bfloat16)
                        ref[spot, pl.ds(row, TILE), pl.ds(bins + lane, LANES)] = (
                            imags[i][j] * scale
                        ).astype(jnp.bfloat16)
        return 0

    lax.fori_loop(0, rows // TILE, one_tile, 0)


def reader(ref, *lead):
    def read(part, w, row, lane):
        index = lead + (part, w, pl.ds(row, TILE), pl.ds(lane, LANES))
        return ref[index].astype(jnp.float32)

    return read


def cross_kernel(position, mine, got, down0, down1, up0, up1, side0, side1, xs, xd, zs, zd, here, chip):
    windows, rows, bins = mine.shape[2], mine.shape[3], mine.shape[4]
    core, x = position[0], position[1]
    run = functools.partial(products, rows=rows, bins=bins, windows=windows)
    own_p = [reader(mine, 0), reader(got, 0)]
    own_q = [reader(mine, 1), reader(got, 1)]
    down = [reader(down0), reader(down1)]
    up = [reader(up0), reader(up1)]
    side = [reader(side0), reader(side1)]

    def spots(straight, crossed, base):
        return [
            [[(straight, base + core)], [(straight, base + 1 - core)]],
            [[(crossed, base + core)], [(crossed, base + 1 - core)]],
        ]

    @pl.when(x == 0)
    def _():
        run(up, own_q, spots(zs, zd, 2))
        run(side, down, spots(xs, xd, 0))
        run(own_p, side, spots(here, chip, 0))
        run(own_p, down, spots(here, chip, 2))

    @pl.when(x == 1)
    def _():
        run(up, side, spots(zs, zd, 0))
        run(up, own_q, spots(zs, zd, 2))
        run(side, own_q, spots(xs, xd, 0))
        run(own_p, down, spots(here, chip, 2))

    for own, spot in ((own_p, 4), (own_q, 5)):
        both = [[(here, spot), (chip, spot)]]

        @pl.when(core == 0)
        def _():
            run([own[0]], [own[1]], [both])

        @pl.when(core == 1)
        def _():
            run([own[1]], [own[0]], [both])


def cross(position, mine, got, received):
    rows, bins = mine.shape[3], mine.shape[4]
    out = lambda n: jax.ShapeDtypeStruct((n, rows, 2 * bins), jnp.bfloat16)
    vmem = pl.BlockSpec(memory_space=pltpu.VMEM)
    return pl.pallas_call(
        cross_kernel,
        out_shape=(out(2), out(2), out(4), out(4), out(6), out(6)),
        in_specs=[pl.BlockSpec(memory_space=pltpu.SMEM)] + [vmem] * 8,
        out_specs=[vmem] * 6,
        compiler_params=pltpu.CompilerParams(vmem_limit_bytes=VMEM_LIMIT),
        cost_estimate=pl.CostEstimate(flops=20_000_000, bytes_accessed=6_000_000, transcendentals=0),
        name="cross",
    )(position, mine, got, *received)


def lag_kernel(position, offsets, limits, here, chip, xs, xd, zs, zd, table, out, cand):
    core, x = position[0], position[1]
    rows, lags = here.shape[1], table.shape[1]
    for near_side, (local, side, far) in enumerate(((here, xs, zs), (chip, xd, zd))):
        half = core if near_side == 0 else 1 - core
        p_rows = pl.ds(pl.multiple_of(half * rows, rows), rows)
        q_rows = pl.ds(pl.multiple_of((2 + half) * rows, rows), rows)
        cand[0, p_rows, :] = local[4]
        cand[0, q_rows, :] = local[5]
        cand[3:5, p_rows, :] = local[2:4]
        cand[3:5, q_rows, :] = far[2:4]

        @pl.when(x == 0)
        def _():
            cand[1:3, p_rows, :] = local[0:2]
            cand[1:3, q_rows, :] = side[...]

        @pl.when(x == 1)
        def _():
            cand[1:3, p_rows, :] = side[...]
            cand[1:3, q_rows, :] = far[0:2]

    lag = lax.broadcasted_iota(jnp.int32, (1, lags), 1)
    distance = jnp.minimum(lag, lags - lag)
    for slot in range(out.shape[1]):
        offset = offsets[0, slot]
        lagged = jnp.dot(
            cand[jnp.clip(offset - 1 + core, 0, 4)],
            table[...],
            preferred_element_type=jnp.float32,
        )
        limit = jnp.where(offset > 0, limits[0, slot], 0)
        out[0, slot] = jnp.where(distance < limit, lagged, 0.0).astype(jnp.bfloat16)


def lag_products(position, offsets, limits, pieces, table):
    rows, width = pieces[0].shape[1:]
    channels, lags = 4 * rows, table.shape[1]
    vmem = pl.BlockSpec(memory_space=pltpu.VMEM)
    smem = pl.BlockSpec(memory_space=pltpu.SMEM)
    return pl.pallas_call(
        lag_kernel,
        out_shape=jax.ShapeDtypeStruct((1, offsets.shape[1], channels, lags), jnp.bfloat16),
        in_specs=[smem] * 3 + [vmem] * 7,
        out_specs=vmem,
        scratch_shapes=[pltpu.VMEM((5, channels, width), jnp.bfloat16)],
        compiler_params=pltpu.CompilerParams(vmem_limit_bytes=VMEM_LIMIT),
        cost_estimate=pl.CostEstimate(flops=500_000_000, bytes_accessed=4_000_000, transcendentals=0),
        name="lags",
    )(position, offsets, limits, *pieces, table)


def phase_table(bins, lag_count):
    freq = np.arange(bins, dtype=np.int64) + BAND_LO
    phase = freq[:, None] * np.arange(lag_count, dtype=np.int64)[None, :] % lag_count
    angle = (2.0 * math.pi / lag_count * phase).astype(np.float32)
    scale = np.float32(1.0 / math.sqrt(bins))
    rows = [np.cos(angle) * scale, -np.sin(angle) * scale]
    return np.concatenate(rows, axis=0).astype(jnp.bfloat16)


def moves(n):
    every = range(n)
    return dict(
        chip=[(i, i ^ 1) for i in every],
        xs=[(i, i ^ 2) for i in every],
        xd=[(i, i ^ 3) for i in every],
        down=[(i, i - 4) for i in every if i >= 4],
        crossed=[(i, (i - 4) ^ 1) for i in every if i >= 4],
        up=[(i, i + 4) for i in every if i + 4 < n],
    )


def local(spectra, pair_offset, lag_limit):
    n = lax.axis_size("pairs")
    move = {name: functools.partial(lax.ppermute, axis_name="pairs", perm=perm) for name, perm in moves(n).items()}
    index = lax.axis_index("pairs")
    core, x = index % 2, index // 2 % 2
    position = jnp.stack([core, x]).astype(jnp.int32)
    mine, theirs = whiten(position, spectra)
    table = jnp.asarray(phase_table(spectra.shape[4], 2 * spectra.shape[4]))

    got = move["chip"](theirs)
    received = {}
    for s, own in enumerate((mine, got)):
        received["down", s] = move["down"](own[0])
        received["up", s] = move["up"](own[1])
        received["side", s] = move["xs"](lax.dynamic_index_in_dim(own, 1 - x, keepdims=False))
    order = [received[name, s] for name in ("down", "up", "side") for s in range(2)]
    xs, xd, zs, zd, here, chip = cross(position, mine, got, order)
    zs = move["down"](zs)
    zd = move["crossed"](zd)
    xs = move["xs"](xs)
    xd = move["xd"](xd)
    chip = move["chip"](chip)
    return lag_products(position, pair_offset, lag_limit, (here, chip, xs, xd, zs, zd), table)


def solution(mesh):
    in_specs = (
        P(("hours", "pairs"), None, None, None, None),
        P(("hours", "pairs"), None),
        P(("hours", "pairs"), None),
    )
    out_specs = P(("hours", "pairs"), None, None, None)
    return jax.shard_map(local, mesh=mesh, in_specs=in_specs, out_specs=out_specs, check_vma=False)
```

```python
import functools
import math

import jax
import jax.numpy as jnp
import numpy as np
from jax import lax
from jax.experimental import pallas as pl
from jax.experimental.pallas import tpu as pltpu
from jax.sharding import PartitionSpec as P

BAND_LO = 16
TILE = 16
LANES = 128
VMEM_LIMIT = 16 * 1024 * 1024
VMEM_ALL = 60 * 1024 * 1024
WHITEN_TILE = 16


def whiten_rows(read, write, windows, rows):
    def one_window(w, _):
        for row in range(0, rows, WHITEN_TILE):
            block = pl.ds(row, WHITEN_TILE)
            values = read(w, block).astype(jnp.float32)
            power = jnp.sum(jnp.sum(values * values, axis=0), axis=-1, keepdims=True)
            power = power / (values.shape[0] * values.shape[-1])
            write(w, block, (values * lax.rsqrt(power + 1e-06)).astype(jnp.bfloat16))
        return 0

    lax.fori_loop(0, windows, one_window, 0)


def quarters_kernel(position, spectra, theirs, side, up, down, sent):
    rows = side.shape[2]
    core, x = position[0], position[1]
    copies = []
    for k, half, target in (
        (0, 1 - core, theirs.at[0]),
        (1, 1 - core, theirs.at[1]),
        (1 - x, core, side),
        (1, core, up),
        (0, core, down),
    ):
        base = pl.multiple_of((2 * k + half) * rows, rows)
        source = spectra.at[0, :, :, pl.ds(base, rows), :]
        copies.append(pltpu.make_async_copy(source, target, sent.at[len(copies)]))
    for copy in copies:
        copy.start()
    for copy in copies:
        copy.wait()


def quarters(position, spectra):
    parts, windows, channels, bins = spectra.shape[1:]
    shape = (parts, windows, channels // 4, bins)
    return pl.pallas_call(
        quarters_kernel,
        out_shape=[jax.ShapeDtypeStruct((2,) + shape, jnp.bfloat16)]
        + [jax.ShapeDtypeStruct(shape, jnp.bfloat16)] * 3,
        in_specs=[pl.BlockSpec(memory_space=pltpu.SMEM), pl.BlockSpec(memory_space=pl.ANY)],
        out_specs=[pl.BlockSpec(memory_space=pltpu.VMEM)] * 4,
        scratch_shapes=[pltpu.SemaphoreType.DMA((5,))],
        compiler_params=pltpu.CompilerParams(vmem_limit_bytes=VMEM_ALL),
        cost_estimate=pl.CostEstimate(flops=1000, bytes_accessed=1000, transcendentals=0),
        name="quarters",
    )(position, spectra)


def whiten_got_kernel(position, got, p_out, q_out, side_out):
    windows, rows = got.shape[2], got.shape[3]
    for k, target in ((0, p_out), (1, q_out)):

        def read(w, block):
            return got[k, :, w, block, :]

        def write(w, block, values):
            target[:, w, block, :] = values

        whiten_rows(read, write, windows, rows)

    @pl.when(position[1] == 0)
    def _():
        side_out[...] = q_out[...]

    @pl.when(position[1] == 1)
    def _():
        side_out[...] = p_out[...]


def whiten_got(position, got):
    vmem = pl.BlockSpec(memory_space=pltpu.VMEM)
    return pl.pallas_call(
        whiten_got_kernel,
        out_shape=[jax.ShapeDtypeStruct(got.shape[1:], jnp.bfloat16)] * 3,
        in_specs=[pl.BlockSpec(memory_space=pltpu.SMEM), vmem],
        out_specs=[vmem] * 3,
        compiler_params=pltpu.CompilerParams(vmem_limit_bytes=VMEM_LIMIT),
        cost_estimate=pl.CostEstimate(flops=3_000_000, bytes_accessed=3_000_000, transcendentals=0),
        name="whiten_got",
    )(position, got)


def whiten_blocks_kernel(*refs):
    count = len(refs) // 2
    for source, target in zip(refs[:count], refs[count:]):

        def read(w, block):
            return source[:, w, block, :]

        def write(w, block, values):
            target[:, w, block, :] = values

        whiten_rows(read, write, source.shape[1], source.shape[2])


def whiten_blocks(*blocks):
    vmem = pl.BlockSpec(memory_space=pltpu.VMEM)
    return pl.pallas_call(
        whiten_blocks_kernel,
        out_shape=[jax.ShapeDtypeStruct(block.shape, jnp.bfloat16) for block in blocks],
        in_specs=[vmem] * len(blocks),
        out_specs=[vmem] * len(blocks),
        compiler_params=pltpu.CompilerParams(vmem_limit_bytes=VMEM_LIMIT),
        cost_estimate=pl.CostEstimate(flops=3_000_000, bytes_accessed=3_000_000, transcendentals=0),
        name="whiten_blocks",
    )(*blocks)


def products(first, second, stores, rows, bins, windows):
    def one_tile(step, _):
        row = pl.multiple_of(step * TILE, TILE)
        for lane in range(0, bins, LANES):
            reals = [[0.0] * len(second) for _ in first]
            imags = [[0.0] * len(second) for _ in first]
            for w in range(windows):
                a = [[f(part, w, row, lane) for part in range(2)] for f in first]
                b = [[f(part, w, row, lane) for part in range(2)] for f in second]
                for i, (ar, ai) in enumerate(a):
                    for j, (br, bi) in enumerate(b):
                        if not stores[i][j]:
                            continue
                        reals[i][j] = reals[i][j] + (ar * br + ai * bi)
                        imags[i][j] = imags[i][j] + (ar * bi - ai * br)
            for i in range(len(first)):
                for j in range(len(second)):
                    for ref, spot in stores[i][j]:
                        scale = 1.0 / windows
                        ref[spot, pl.ds(row, TILE), pl.ds(lane, LANES)] = (
                            reals[i][j] * scale
                        ).astype(jnp.bfloat16)
                        ref[spot, pl.ds(row, TILE), pl.ds(bins + lane, LANES)] = (
                            imags[i][j] * scale
                        ).astype(jnp.bfloat16)
        return 0

    lax.fori_loop(0, rows // TILE, one_tile, 0)


def reader(ref, *lead):
    def read(part, w, row, lane):
        index = lead + (part, w, pl.ds(row, TILE), pl.ds(lane, LANES))
        return ref[index].astype(jnp.float32)

    return read


def spots(core, straight, crossed, base):
    return [
        [[(straight, base + core)], [(straight, base + 1 - core)]],
        [[(crossed, base + core)], [(crossed, base + 1 - core)]],
    ]


def chip_kernel(position, mine_p, got_p, mine_q, got_q, here, chip):
    windows, rows, bins = mine_q.shape[1:]
    core = position[0]
    run = functools.partial(products, rows=rows, bins=bins, windows=windows)
    for spot, own in enumerate(((mine_p, got_p), (mine_q, got_q))):
        both = [[(here, spot), (chip, spot)]]

        @pl.when(core == 0)
        def _():
            run([reader(own[0])], [reader(own[1])], [both])

        @pl.when(core == 1)
        def _():
            run([reader(own[1])], [reader(own[0])], [both])


def back_kernel(position, mine_p, got_p, mine_q, got_q, up0, up1, side0, side1, zs, zd, here, chip):
    windows, rows, bins = mine_q.shape[1:]
    core, x = position[0], position[1]
    run = functools.partial(products, rows=rows, bins=bins, windows=windows)
    up = [reader(up0), reader(up1)]
    side = [reader(side0), reader(side1)]

    run(up, [reader(mine_q), reader(got_q)], spots(core, zs, zd, 2))

    @pl.when(x == 0)
    def _():
        run([reader(mine_p), reader(got_p)], side, spots(core, here, chip, 0))

    @pl.when(x == 1)
    def _():
        run(up, side, spots(core, zs, zd, 0))


def near_kernel(position, mine_q, got_q, down0, down1, side0, side1, after, xs, xd):
    windows, rows, bins = mine_q.shape[1:]
    core, x = position[0], position[1]
    run = functools.partial(products, rows=rows, bins=bins, windows=windows)
    side = [reader(side0), reader(side1)]

    @pl.when(x == 0)
    def _():
        run(side, [reader(down0), reader(down1)], spots(core, xs, xd, 0))

    @pl.when(x == 1)
    def _():
        run(side, [reader(mine_q), reader(got_q)], spots(core, xs, xd, 0))


def far_kernel(position, mine_p, got_p, down0, down1, after, here, chip):
    windows, rows, bins = mine_p.shape[1:]
    run = functools.partial(products, rows=rows, bins=bins, windows=windows)
    own = [reader(mine_p), reader(got_p)]
    run(own, [reader(down0), reader(down1)], spots(position[0], here, chip, 0))


def cross(kernel, counts, position, *blocks, after=()):
    rows, bins = blocks[0].shape[2:]
    vmem = pl.BlockSpec(memory_space=pltpu.VMEM)
    return pl.pallas_call(
        kernel,
        out_shape=[jax.ShapeDtypeStruct((n, rows, 2 * bins), jnp.bfloat16) for n in counts],
        in_specs=[pl.BlockSpec(memory_space=pltpu.SMEM)]
        + [vmem] * len(blocks)
        + [pl.BlockSpec(memory_space=pl.ANY)] * len(after),
        out_specs=[vmem] * len(counts),
        compiler_params=pltpu.CompilerParams(vmem_limit_bytes=VMEM_LIMIT),
        cost_estimate=pl.CostEstimate(flops=10_000_000, bytes_accessed=5_000_000, transcendentals=0),
        name=kernel.__name__,
    )(position, *blocks, *after)


def lag_kernel(position, offsets, limits, *refs):
    table, out, cand = refs[10:]
    core, x = position[0], position[1]
    rows, lags = refs[0].shape[1], table.shape[1]
    for half, pieces in ((core, refs[:5]), (1 - core, refs[5:10])):
        pair, near, far, side, back = pieces
        p_rows = pl.ds(pl.multiple_of(half * rows, rows), rows)
        q_rows = pl.ds(pl.multiple_of((2 + half) * rows, rows), rows)
        cand[0, p_rows, :] = pair[0]
        cand[0, q_rows, :] = pair[1]
        cand[3:5, p_rows, :] = far[...]
        cand[3:5, q_rows, :] = back[2:4]

        @pl.when(x == 0)
        def _():
            cand[1:3, p_rows, :] = near[...]
            cand[1:3, q_rows, :] = side[...]

        @pl.when(x == 1)
        def _():
            cand[1:3, p_rows, :] = side[...]
            cand[1:3, q_rows, :] = back[0:2]

    lag = lax.broadcasted_iota(jnp.int32, (1, lags), 1)
    distance = jnp.minimum(lag, lags - lag)
    for slot in range(out.shape[1]):
        offset = offsets[0, slot]
        lagged = jnp.dot(
            cand[jnp.clip(offset - 1 + core, 0, 4)],
            table[...],
            preferred_element_type=jnp.float32,
        )
        limit = jnp.where(offset > 0, limits[0, slot], 0)
        out[0, slot] = jnp.where(distance < limit, lagged, 0.0).astype(jnp.bfloat16)


def lag_products(position, offsets, limits, sides, table):
    pieces = sides[0] + sides[1]
    rows, width = pieces[0].shape[1:]
    channels, lags = 4 * rows, table.shape[1]
    vmem = pl.BlockSpec(memory_space=pltpu.VMEM)
    smem = pl.BlockSpec(memory_space=pltpu.SMEM)
    return pl.pallas_call(
        lag_kernel,
        out_shape=jax.ShapeDtypeStruct((1, offsets.shape[1], channels, lags), jnp.bfloat16),
        in_specs=[smem] * 3 + [vmem] * (len(pieces) + 1),
        out_specs=vmem,
        scratch_shapes=[pltpu.VMEM((5, channels, width), jnp.bfloat16)],
        compiler_params=pltpu.CompilerParams(vmem_limit_bytes=VMEM_LIMIT),
        cost_estimate=pl.CostEstimate(flops=500_000_000, bytes_accessed=4_000_000, transcendentals=0),
        name="lags",
    )(position, offsets, limits, *pieces, table)


def phase_table(bins, lag_count):
    freq = np.arange(bins, dtype=np.int64) + BAND_LO
    phase = freq[:, None] * np.arange(lag_count, dtype=np.int64)[None, :] % lag_count
    angle = (2.0 * math.pi / lag_count * phase).astype(np.float32)
    scale = np.float32(1.0 / math.sqrt(bins))
    rows = [np.cos(angle) * scale, -np.sin(angle) * scale]
    return np.concatenate(rows, axis=0).astype(jnp.bfloat16)


def moves(n):
    every = range(n)
    return dict(
        chip=[(i, i ^ 1) for i in every],
        xs=[(i, i ^ 2) for i in every],
        xd=[(i, i ^ 3) for i in every],
        down=[(i, i - 4) for i in every if i >= 4],
        crossed=[(i, (i - 4) ^ 1) for i in every if i >= 4],
        up=[(i, i + 4) for i in every if i + 4 < n],
    )


def local(spectra, pair_offset, lag_limit):
    n = lax.axis_size("pairs")
    move = {name: functools.partial(lax.ppermute, axis_name="pairs", perm=perm) for name, perm in moves(n).items()}
    index = lax.axis_index("pairs")
    core, x = index % 2, index // 2 % 2
    position = jnp.stack([core, x]).astype(jnp.int32)
    table = jnp.asarray(phase_table(spectra.shape[4], 2 * spectra.shape[4]))

    theirs, side_raw, up_raw, down_raw = quarters(position, spectra)
    got = move["chip"](theirs)
    side0 = move["xs"](side_raw)
    up0 = move["up"](up_raw)
    down0 = move["down"](down_raw)
    got_p, got_q, got_side = whiten_got(position, got)
    side1 = move["xs"](got_side)
    up1 = move["up"](got_q)
    down1 = move["down"](got_p)
    mine_p, mine_q = whiten_blocks(down_raw, up_raw)
    side0, up0, down0 = whiten_blocks(side0, up0, down0)

    own = (mine_p, got_p, mine_q, got_q)
    pair_here, pair_chip = cross(chip_kernel, (2, 2), position, *own)
    pair_chip = move["chip"](pair_chip)

    zs, zd, near_here, near_chip = cross(
        back_kernel, (4, 4, 2, 2), position, *own, up0, up1, side0, side1
    )
    xs, xd = cross(
        near_kernel, (2, 2), position, mine_q, got_q, down0, down1, side0, side1, after=(zd,)
    )
    far_here, far_chip = cross(
        far_kernel, (2, 2), position, mine_p, got_p, down0, down1, after=(xd,)
    )
    zs = move["down"](zs)
    zd = move["crossed"](zd)
    near_chip = move["chip"](near_chip)
    xs = move["xs"](xs)
    xd = move["xd"](xd)
    far_chip = move["chip"](far_chip)
    sides = ((pair_here, near_here, far_here, xs, zs), (pair_chip, near_chip, far_chip, xd, zd))
    return lag_products(position, pair_offset, lag_limit, sides, table)


def solution(mesh):
    in_specs = (
        P(("hours", "pairs"), None, None, None, None),
        P(("hours", "pairs"), None),
        P(("hours", "pairs"), None),
    )
    out_specs = P(("hours", "pairs"), None, None, None)
    return jax.shard_map(local, mesh=mesh, in_specs=in_specs, out_specs=out_specs, check_vma=False)
```

```python
import functools
import math

import jax
import jax.numpy as jnp
import numpy as np
from jax import lax
from jax.experimental import pallas as pl
from jax.experimental.pallas import tpu as pltpu
from jax.sharding import PartitionSpec as P

BAND_LO = 16
TILE = 16
LANES = 128
VMEM_LIMIT = 16 * 1024 * 1024
VMEM_ALL = 16 * 1024 * 1024
WHITEN_TILE = 16

SMALL = pl.CostEstimate(flops=1000, bytes_accessed=1000, transcendentals=0)
LARGE = pl.CostEstimate(flops=10_000_000_000, bytes_accessed=40_000_000, transcendentals=0)
OUT_SPACE = pl.ANY


def whiten_rows(read, write, windows, rows):
    def one_window(w, _):
        for row in range(0, rows, WHITEN_TILE):
            block = pl.ds(row, WHITEN_TILE)
            values = read(w, block).astype(jnp.float32)
            power = jnp.sum(jnp.sum(values * values, axis=0), axis=-1, keepdims=True)
            power = power / (values.shape[0] * values.shape[-1])
            write(w, block, (values * lax.rsqrt(power + 1e-06)).astype(jnp.bfloat16))
        return 0

    lax.fori_loop(0, windows, one_window, 0)


def place():
    index = lax.axis_index("pairs")
    return lax.rem(index, 2), lax.rem(lax.div(index, 2), 2)


def quarters_kernel(spectra, theirs, side, up, down, sent):
    rows = side.shape[2]
    core, x = place()
    copies = []
    for k, half, target in (
        (0, core, down),
        (1, core, up),
        (1 - x, core, side),
        (0, 1 - core, theirs.at[0]),
        (1, 1 - core, theirs.at[1]),
    ):
        base = pl.multiple_of((2 * k + half) * rows, rows)
        source = spectra.at[0, :, :, pl.ds(base, rows), :]
        copies.append(pltpu.make_async_copy(source, target, sent.at[len(copies)]))
    for copy in copies:
        copy.start()
    for copy in copies:
        copy.wait()


def quarters(spectra):
    parts, windows, channels, bins = spectra.shape[1:]
    shape = (parts, windows, channels // 4, bins)
    return pl.pallas_call(
        quarters_kernel,
        out_shape=[jax.ShapeDtypeStruct((2,) + shape, jnp.bfloat16)]
        + [jax.ShapeDtypeStruct(shape, jnp.bfloat16)] * 3,
        in_specs=[pl.BlockSpec(memory_space=pl.ANY)],
        out_specs=[pl.BlockSpec(memory_space=OUT_SPACE)] * 4,
        scratch_shapes=[pltpu.SemaphoreType.DMA((5,))],
        compiler_params=pltpu.CompilerParams(vmem_limit_bytes=VMEM_ALL),
        cost_estimate=SMALL,
        name="quarters",
    )(spectra)


def whiten_got_kernel(got, p_out, q_out, side_out):
    windows, rows = got.shape[2], got.shape[3]
    _, x = place()
    for k, target in ((0, p_out), (1, q_out)):

        def read(w, block):
            return got[k, :, w, block, :]

        def write(w, block, values):
            target[:, w, block, :] = values

        whiten_rows(read, write, windows, rows)

    @pl.when(x == 0)
    def _():
        side_out[...] = q_out[...]

    @pl.when(x == 1)
    def _():
        side_out[...] = p_out[...]


def whiten_got(got):
    vmem = pl.BlockSpec(memory_space=pltpu.VMEM)
    return pl.pallas_call(
        whiten_got_kernel,
        out_shape=[jax.ShapeDtypeStruct(got.shape[1:], jnp.bfloat16)] * 3,
        in_specs=[vmem],
        out_specs=[vmem] * 3,
        compiler_params=pltpu.CompilerParams(vmem_limit_bytes=VMEM_LIMIT),
        cost_estimate=SMALL,
        name="whiten_got",
    )(got)


def whiten_block_kernel(source, *rest):
    target = rest[-1]

    def read(w, block):
        return source[:, w, block, :]

    def write(w, block, values):
        target[:, w, block, :] = values

    whiten_rows(read, write, source.shape[1], source.shape[2])


def whiten_block(block, after=None):
    vmem = pl.BlockSpec(memory_space=pltpu.VMEM)
    extra = [] if after is None else [after]
    return pl.pallas_call(
        whiten_block_kernel,
        out_shape=jax.ShapeDtypeStruct(block.shape, jnp.bfloat16),
        in_specs=[vmem] + [pl.BlockSpec(memory_space=pl.ANY)] * len(extra),
        out_specs=vmem,
        compiler_params=pltpu.CompilerParams(vmem_limit_bytes=VMEM_LIMIT),
        cost_estimate=SMALL,
        name="whiten_block",
    )(block, *extra)


def products(first, second, stores, rows, bins, windows):
    def one_tile(step, _):
        row = pl.multiple_of(step * TILE, TILE)
        for lane in range(0, bins, LANES):
            reals = [[0.0] * len(second) for _ in first]
            imags = [[0.0] * len(second) for _ in first]
            for w in range(windows):
                a = [[f(part, w, row, lane) for part in range(2)] for f in first]
                b = [[f(part, w, row, lane) for part in range(2)] for f in second]
                for i, (ar, ai) in enumerate(a):
                    for j, (br, bi) in enumerate(b):
                        if not stores[i][j]:
                            continue
                        reals[i][j] = reals[i][j] + (ar * br + ai * bi)
                        imags[i][j] = imags[i][j] + (ar * bi - ai * br)
            for i in range(len(first)):
                for j in range(len(second)):
                    for ref, spot in stores[i][j]:
                        scale = 1.0 / windows
                        ref[spot, pl.ds(row, TILE), pl.ds(lane, LANES)] = (
                            reals[i][j] * scale
                        ).astype(jnp.bfloat16)
                        ref[spot, pl.ds(row, TILE), pl.ds(bins + lane, LANES)] = (
                            imags[i][j] * scale
                        ).astype(jnp.bfloat16)
        return 0

    lax.fori_loop(0, rows // TILE, one_tile, 0)


def reader(ref, *lead):
    def read(part, w, row, lane):
        index = lead + (part, w, pl.ds(row, TILE), pl.ds(lane, LANES))
        return ref[index].astype(jnp.float32)

    return read


def spots(core, ref, base):
    return [[(ref, base + core)], [(ref, base + 1 - core)]]


def chip_kernel(mine_p, got_p, mine_q, got_q, pair):
    windows, rows, bins = mine_q.shape[1:]
    core, _ = place()
    run = functools.partial(products, rows=rows, bins=bins, windows=windows)
    for spot, own in enumerate(((mine_p, got_p), (mine_q, got_q))):
        both = [[(pair, spot)]]

        @pl.when(core == 0)
        def _():
            run([reader(own[0])], [reader(own[1])], [both])

        @pl.when(core == 1)
        def _():
            run([reader(own[1])], [reader(own[0])], [both])


def back_kernel(mine_q, got_q, up, side0, side1, after, back):
    windows, rows, bins = mine_q.shape[1:]
    core, x = place()
    run = functools.partial(products, [reader(up)], rows=rows, bins=bins, windows=windows)
    run([reader(mine_q), reader(got_q)], [spots(core, back, 2)])

    @pl.when(x == 1)
    def _():
        run([reader(side0), reader(side1)], [spots(core, back, 0)])


def near_kernel(mine_q, got_q, down0, down1, side0, side1, after, xs, xd):
    windows, rows, bins = mine_q.shape[1:]
    core, x = place()
    side = [reader(side0), reader(side1)]
    stores = [spots(core, xs, 0), spots(core, xd, 0)]
    run = functools.partial(products, side, rows=rows, bins=bins, windows=windows)

    @pl.when(x == 0)
    def _():
        run([reader(down0), reader(down1)], stores)

    @pl.when(x == 1)
    def _():
        run([reader(mine_q), reader(got_q)], stores)


def own_kernel(mine_p, got_p, down0, down1, side0, side1, pair, after, here, chip):
    here[4:6] = pair[...]
    chip[4:6] = pair[...]
    windows, rows, bins = mine_p.shape[1:]
    core, x = place()
    own = [reader(mine_p), reader(got_p)]
    run = functools.partial(products, own, rows=rows, bins=bins, windows=windows)
    run([reader(down0), reader(down1)], [spots(core, here, 2), spots(core, chip, 2)])

    @pl.when(x == 0)
    def _():
        run([reader(side0), reader(side1)], [spots(core, here, 0), spots(core, chip, 0)])


def cross(kernel, counts, *blocks, after=None):
    rows, bins = blocks[0].shape[2:]
    extra = [] if after is None else [after]
    vmem = pl.BlockSpec(memory_space=pltpu.VMEM)
    return pl.pallas_call(
        kernel,
        out_shape=[jax.ShapeDtypeStruct((n, rows, 2 * bins), jnp.bfloat16) for n in counts],
        in_specs=[vmem] * len(blocks) + [pl.BlockSpec(memory_space=pl.ANY)] * len(extra),
        out_specs=[vmem] * len(counts),
        compiler_params=pltpu.CompilerParams(vmem_limit_bytes=VMEM_LIMIT),
        cost_estimate=SMALL,
        name=kernel.__name__,
    )(*blocks, *extra)


def lag_kernel(flip, offsets, limits, own, side, back, table, earlier, out, cand, lagged, sent):
    core, x = place()
    half = core if flip == 0 else 1 - core
    rows, lags = own.shape[1], table.shape[1]
    p_rows, q_rows = pl.ds(0, rows), pl.ds(rows, rows)
    cand[0, p_rows, :] = own[4]
    cand[0, q_rows, :] = own[5]
    cand[3:5, p_rows, :] = own[2:4]
    cand[3:5, q_rows, :] = back[2:4]

    @pl.when(x == 0)
    def _():
        cand[1:3, p_rows, :] = own[0:2]
        cand[1:3, q_rows, :] = side[...]

    @pl.when(x == 1)
    def _():
        cand[1:3, p_rows, :] = side[...]
        cand[1:3, q_rows, :] = back[0:2]

    lag = lax.broadcasted_iota(jnp.int32, (1, lags), 1)
    distance = jnp.minimum(lag, lags - lag)
    copies = []
    for slot in range(out.shape[1]):
        offset = offsets[0, slot]
        product = jnp.dot(
            cand[jnp.clip(offset - 1 + core, 0, 4)],
            table[...],
            preferred_element_type=jnp.float32,
        )
        limit = jnp.where(offset > 0, limits[0, slot], 0)
        lagged[slot] = jnp.where(distance < limit, product, 0.0).astype(jnp.bfloat16)
        for k in range(2):
            target = pl.multiple_of((2 * k + half) * rows, rows)
            copies.append(
                pltpu.make_async_copy(
                    lagged.at[slot, pl.ds(k * rows, rows), :],
                    out.at[0, slot, pl.ds(target, rows), :],
                    sent.at[slot, k],
                )
            )
            copies[-1].start()
    for copy in copies:
        copy.wait()


def lag_products(flip, cost, offsets, limits, pieces, table, earlier):
    rows, width = pieces[0].shape[1:]
    slots, lags = offsets.shape[1], table.shape[1]
    vmem = pl.BlockSpec(memory_space=pltpu.VMEM)
    smem = pl.BlockSpec(memory_space=pltpu.SMEM)
    kernel = functools.partial(lag_kernel, flip)
    extra = [earlier]
    if earlier is None:
        kernel = lambda *refs: lag_kernel(flip, *refs[:6], None, *refs[6:])
        extra = []
    return pl.pallas_call(
        kernel,
        out_shape=jax.ShapeDtypeStruct((1, slots, 4 * rows, lags), jnp.bfloat16),
        in_specs=[smem] * 2 + [vmem] * 4 + [pl.BlockSpec(memory_space=pl.ANY)] * len(extra),
        out_specs=pl.BlockSpec(memory_space=pl.ANY),
        scratch_shapes=[
            pltpu.VMEM((5, 2 * rows, width), jnp.bfloat16),
            pltpu.VMEM((slots, 2 * rows, lags), jnp.bfloat16),
            pltpu.SemaphoreType.DMA((slots, 2)),
        ],
        input_output_aliases={6: 0} if extra else {},
        compiler_params=pltpu.CompilerParams(vmem_limit_bytes=VMEM_LIMIT),
        cost_estimate=cost,
        name="lags",
    )(offsets, limits, *pieces, table, *extra)


def phase_table(bins, lag_count):
    freq = np.arange(bins, dtype=np.int64) + BAND_LO
    phase = freq[:, None] * np.arange(lag_count, dtype=np.int64)[None, :] % lag_count
    angle = (2.0 * math.pi / lag_count * phase).astype(np.float32)
    scale = np.float32(1.0 / math.sqrt(bins))
    rows = [np.cos(angle) * scale, -np.sin(angle) * scale]
    return np.concatenate(rows, axis=0).astype(jnp.bfloat16)


def moves(n):
    every = range(n)
    return dict(
        chip=[(i, i ^ 1) for i in every],
        xs=[(i, i ^ 2) for i in every],
        xd=[(i, i ^ 3) for i in every],
        down=[(i, i - 4) for i in every if i >= 4],
        crossed=[(i, (i - 4) ^ 1) for i in every if i >= 4],
        up=[(i, i + 4) for i in every if i + 4 < n],
    )


def local(spectra, pair_offset, lag_limit):
    n = lax.axis_size("pairs")
    move = {name: functools.partial(lax.ppermute, axis_name="pairs", perm=perm) for name, perm in moves(n).items()}
    table = jnp.asarray(phase_table(spectra.shape[4], 2 * spectra.shape[4]))

    theirs, side_raw, up_raw, down_raw = quarters(spectra)
    got = move["chip"](theirs)
    down0 = move["down"](down_raw)
    side0 = move["xs"](side_raw)
    up0 = move["up"](up_raw)
    got_p, got_q, got_side = whiten_got(got)
    down1 = move["down"](got_p)
    side1 = move["xs"](got_side)
    up1 = move["up"](got_q)
    mine_p = whiten_block(down_raw)
    mine_q = whiten_block(up_raw)
    (pair,) = cross(chip_kernel, (2,), mine_p, got_p, mine_q, got_q)
    down0 = whiten_block(down0, after=pair)
    side0 = whiten_block(side0, after=down0)
    up0 = whiten_block(up0, after=side0)

    (zs,) = cross(back_kernel, (4,), mine_q, got_q, up0, side0, side1, after=up0)
    xs, xd = cross(near_kernel, (2, 2), mine_q, got_q, down0, down1, side0, side1, after=zs)
    own_here, own_chip = cross(
        own_kernel, (6, 6), mine_p, got_p, down0, down1, side0, side1, pair, after=xd
    )
    (zd,) = cross(back_kernel, (4,), mine_q, got_q, up1, side0, side1, after=own_chip)
    zs = move["down"](zs)
    xs = move["xs"](xs)
    xd = move["xd"](xd)
    own_chip = move["chip"](own_chip)
    zd = move["crossed"](zd)
    straight = (own_here, xs, zs)
    crossed = (own_chip, xd, zd)
    out = lag_products(0, LARGE, pair_offset, lag_limit, straight, table, None)
    return lag_products(1, SMALL, pair_offset, lag_limit, crossed, table, out)


def solution(mesh):
    in_specs = (
        P(("hours", "pairs"), None, None, None, None),
        P(("hours", "pairs"), None),
        P(("hours", "pairs"), None),
    )
    out_specs = P(("hours", "pairs"), None, None, None)
    return jax.shard_map(local, mesh=mesh, in_specs=in_specs, out_specs=out_specs, check_vma=False)
```

```python
import functools
import math

import jax
import jax.numpy as jnp
import numpy as np
from jax import lax
from jax.experimental import pallas as pl
from jax.experimental.pallas import tpu as pltpu
from jax.sharding import PartitionSpec as P

BAND_LO = 16
TILE = 16
LANES = 128
VMEM_LIMIT = 16 * 1024 * 1024
VMEM_ALL = 50 * 1024 * 1024
WHITEN_TILE = 16

SMALL = pl.CostEstimate(flops=1000, bytes_accessed=1000, transcendentals=0)
LARGE = pl.CostEstimate(flops=10_000_000_000, bytes_accessed=40_000_000, transcendentals=0)
OUT_SPACE = pl.ANY


def whiten_rows(read, write, windows, rows):
    def one_window(w, _):
        for row in range(0, rows, WHITEN_TILE):
            block = pl.ds(row, WHITEN_TILE)
            values = read(w, block).astype(jnp.float32)
            power = jnp.sum(jnp.sum(values * values, axis=0), axis=-1, keepdims=True)
            power = power / (values.shape[0] * values.shape[-1])
            write(w, block, (values * lax.rsqrt(power + 1e-06)).astype(jnp.bfloat16))
        return 0

    lax.fori_loop(0, windows, one_window, 0)


def place():
    index = lax.axis_index("pairs")
    return lax.rem(index, 2), lax.rem(lax.div(index, 2), 2)


def quarters_kernel(spectra, theirs, side, up, down, sent):
    rows = side.shape[2]
    core, x = place()
    copies = []
    for k, half, target in (
        (0, core, down),
        (1, core, up),
        (1 - x, core, side),
        (0, 1 - core, theirs.at[0]),
        (1, 1 - core, theirs.at[1]),
    ):
        base = pl.multiple_of((2 * k + half) * rows, rows)
        source = spectra.at[0, :, :, pl.ds(base, rows), :]
        copies.append(pltpu.make_async_copy(source, target, sent.at[len(copies)]))
    for copy in copies:
        copy.start()
    for copy in copies:
        copy.wait()


def quarters(spectra):
    parts, windows, channels, bins = spectra.shape[1:]
    shape = (parts, windows, channels // 4, bins)
    return pl.pallas_call(
        quarters_kernel,
        out_shape=[jax.ShapeDtypeStruct((2,) + shape, jnp.bfloat16)]
        + [jax.ShapeDtypeStruct(shape, jnp.bfloat16)] * 3,
        in_specs=[pl.BlockSpec(memory_space=pl.ANY)],
        out_specs=[pl.BlockSpec(memory_space=OUT_SPACE)] * 4,
        scratch_shapes=[pltpu.SemaphoreType.DMA((5,))],
        compiler_params=pltpu.CompilerParams(vmem_limit_bytes=VMEM_ALL),
        cost_estimate=SMALL,
        name="quarters",
    )(spectra)


def whiten_got_kernel(got, p_out, q_out, side_out):
    windows, rows = got.shape[2], got.shape[3]
    _, x = place()
    for k, target in ((0, p_out), (1, q_out)):

        def read(w, block):
            return got[k, :, w, block, :]

        def write(w, block, values):
            target[:, w, block, :] = values

        whiten_rows(read, write, windows, rows)

    @pl.when(x == 0)
    def _():
        side_out[...] = q_out[...]

    @pl.when(x == 1)
    def _():
        side_out[...] = p_out[...]


def whiten_got(got):
    vmem = pl.BlockSpec(memory_space=pltpu.VMEM)
    return pl.pallas_call(
        whiten_got_kernel,
        out_shape=[jax.ShapeDtypeStruct(got.shape[1:], jnp.bfloat16)] * 3,
        in_specs=[vmem],
        out_specs=[vmem] * 3,
        compiler_params=pltpu.CompilerParams(vmem_limit_bytes=VMEM_LIMIT),
        cost_estimate=SMALL,
        name="whiten_got",
    )(got)


def whiten_block_kernel(source, *rest):
    target = rest[-1]

    def read(w, block):
        return source[:, w, block, :]

    def write(w, block, values):
        target[:, w, block, :] = values

    whiten_rows(read, write, source.shape[1], source.shape[2])


def whiten_block(block, after=None):
    vmem = pl.BlockSpec(memory_space=pltpu.VMEM)
    extra = [] if after is None else [after]
    return pl.pallas_call(
        whiten_block_kernel,
        out_shape=jax.ShapeDtypeStruct(block.shape, jnp.bfloat16),
        in_specs=[vmem] + [pl.BlockSpec(memory_space=pl.ANY)] * len(extra),
        out_specs=vmem,
        compiler_params=pltpu.CompilerParams(vmem_limit_bytes=VMEM_LIMIT),
        cost_estimate=SMALL,
        name="whiten_block",
    )(block, *extra)


def products(first, second, stores, rows, bins, windows):
    def one_tile(step, _):
        row = pl.multiple_of(step * TILE, TILE)
        for lane in range(0, bins, LANES):
            reals = [[0.0] * len(second) for _ in first]
            imags = [[0.0] * len(second) for _ in first]
            for w in range(windows):
                a = [[f(part, w, row, lane) for part in range(2)] for f in first]
                b = [[f(part, w, row, lane) for part in range(2)] for f in second]
                for i, (ar, ai) in enumerate(a):
                    for j, (br, bi) in enumerate(b):
                        if not stores[i][j]:
                            continue
                        reals[i][j] = reals[i][j] + (ar * br + ai * bi)
                        imags[i][j] = imags[i][j] + (ar * bi - ai * br)
            for i in range(len(first)):
                for j in range(len(second)):
                    for ref, spot in stores[i][j]:
                        scale = 1.0 / windows
                        ref[spot, pl.ds(row, TILE), pl.ds(lane, LANES)] = (
                            reals[i][j] * scale
                        ).astype(jnp.bfloat16)
                        ref[spot, pl.ds(row, TILE), pl.ds(bins + lane, LANES)] = (
                            imags[i][j] * scale
                        ).astype(jnp.bfloat16)
        return 0

    lax.fori_loop(0, rows // TILE, one_tile, 0)


def reader(ref, *lead):
    def read(part, w, row, lane):
        index = lead + (part, w, pl.ds(row, TILE), pl.ds(lane, LANES))
        return ref[index].astype(jnp.float32)

    return read


def spots(core, ref, base):
    return [[(ref, base + core)], [(ref, base + 1 - core)]]


def chip_kernel(mine_p, got_p, mine_q, got_q, pair):
    windows, rows, bins = mine_q.shape[1:]
    core, _ = place()
    run = functools.partial(products, rows=rows, bins=bins, windows=windows)
    for spot, own in enumerate(((mine_p, got_p), (mine_q, got_q))):
        both = [[(pair, spot)]]

        @pl.when(core == 0)
        def _():
            run([reader(own[0])], [reader(own[1])], [both])

        @pl.when(core == 1)
        def _():
            run([reader(own[1])], [reader(own[0])], [both])


def back_kernel(mine_q, got_q, up, side0, side1, after, back):
    windows, rows, bins = mine_q.shape[1:]
    core, x = place()
    run = functools.partial(products, [reader(up)], rows=rows, bins=bins, windows=windows)
    run([reader(mine_q), reader(got_q)], [spots(core, back, 2)])

    @pl.when(x == 1)
    def _():
        run([reader(side0), reader(side1)], [spots(core, back, 0)])


def near_kernel(mine_q, got_q, down0, down1, side0, side1, after, xs, xd):
    windows, rows, bins = mine_q.shape[1:]
    core, x = place()
    side = [reader(side0), reader(side1)]
    stores = [spots(core, xs, 0), spots(core, xd, 0)]
    run = functools.partial(products, side, rows=rows, bins=bins, windows=windows)

    @pl.when(x == 0)
    def _():
        run([reader(down0), reader(down1)], stores)

    @pl.when(x == 1)
    def _():
        run([reader(mine_q), reader(got_q)], stores)


def own_kernel(mine_p, got_p, down0, down1, side0, side1, pair, after, here, chip):
    here[4:6] = pair[...]
    chip[4:6] = pair[...]
    windows, rows, bins = mine_p.shape[1:]
    core, x = place()
    own = [reader(mine_p), reader(got_p)]
    run = functools.partial(products, own, rows=rows, bins=bins, windows=windows)
    run([reader(down0), reader(down1)], [spots(core, here, 2), spots(core, chip, 2)])

    @pl.when(x == 0)
    def _():
        run([reader(side0), reader(side1)], [spots(core, here, 0), spots(core, chip, 0)])


def cross(kernel, counts, *blocks, after=None):
    rows, bins = blocks[0].shape[2:]
    extra = [] if after is None else [after]
    vmem = pl.BlockSpec(memory_space=pltpu.VMEM)
    return pl.pallas_call(
        kernel,
        out_shape=[jax.ShapeDtypeStruct((n, rows, 2 * bins), jnp.bfloat16) for n in counts],
        in_specs=[vmem] * len(blocks) + [pl.BlockSpec(memory_space=pl.ANY)] * len(extra),
        out_specs=[vmem] * len(counts),
        compiler_params=pltpu.CompilerParams(vmem_limit_bytes=VMEM_LIMIT),
        cost_estimate=SMALL,
        name=kernel.__name__,
    )(*blocks, *extra)


def lag_kernel(flip, classes, offsets, limits, own, side, back, table, out, cand, lagged, sent):
    core, x = place()
    half = core if flip == 0 else 1 - core
    rows, lags = own.shape[1], table.shape[1]
    for spot, k in enumerate(classes):
        part = pl.ds(spot * rows, rows)
        cand[0, part, :] = own[4 + k]
        cand[3:5, part, :] = own[2:4] if k == 0 else back[2:4]

        @pl.when(x == 0)
        def _():
            cand[1:3, part, :] = own[0:2] if k == 0 else side[...]

        @pl.when(x == 1)
        def _():
            cand[1:3, part, :] = side[...] if k == 0 else back[0:2]

    lag = lax.broadcasted_iota(jnp.int32, (1, lags), 1)
    distance = jnp.minimum(lag, lags - lag)
    copies = []
    for slot in range(out.shape[1]):
        offset = offsets[0, slot]
        product = jnp.dot(
            cand[jnp.clip(offset - 1 + core, 0, 4)],
            table[...],
            preferred_element_type=jnp.float32,
        )
        limit = jnp.where(offset > 0, limits[0, slot], 0)
        lagged[slot] = jnp.where(distance < limit, product, 0.0).astype(jnp.bfloat16)
        for spot, k in enumerate(classes):
            target = pl.multiple_of((2 * k + half) * rows, rows)
            copies.append(
                pltpu.make_async_copy(
                    lagged.at[slot, pl.ds(spot * rows, rows), :],
                    out.at[0, slot, pl.ds(target, rows), :],
                    sent.at[slot, spot],
                )
            )
            copies[-1].start()
    for copy in copies:
        copy.wait()


def lag_products(flip, classes, cost, offsets, limits, own, side, back, table, earlier):
    rows, width = own.shape[1:]
    slots, lags = offsets.shape[1], table.shape[1]
    vmem = pl.BlockSpec(memory_space=pltpu.VMEM)
    smem = pl.BlockSpec(memory_space=pltpu.SMEM)
    pieces = [own, side] + ([] if back is None else [back]) + [table]
    extra = [] if earlier is None else [earlier]

    def kernel(*refs):
        refs = list(refs)
        if earlier is not None:
            del refs[2 + len(pieces)]
        if back is None:
            refs.insert(4, None)
        lag_kernel(flip, classes, *refs)

    return pl.pallas_call(
        kernel,
        out_shape=jax.ShapeDtypeStruct((1, slots, 4 * rows, lags), jnp.bfloat16),
        in_specs=[smem] * 2
        + [vmem] * len(pieces)
        + [pl.BlockSpec(memory_space=pl.ANY)] * len(extra),
        out_specs=pl.BlockSpec(memory_space=pl.ANY),
        scratch_shapes=[
            pltpu.VMEM((5, len(classes) * rows, width), jnp.bfloat16),
            pltpu.VMEM((slots, len(classes) * rows, lags), jnp.bfloat16),
            pltpu.SemaphoreType.DMA((slots, len(classes))),
        ],
        input_output_aliases={2 + len(pieces): 0} if extra else {},
        compiler_params=pltpu.CompilerParams(vmem_limit_bytes=VMEM_LIMIT),
        cost_estimate=cost,
        name="lags",
    )(offsets, limits, *pieces, *extra)


def phase_table(bins, lag_count):
    freq = np.arange(bins, dtype=np.int64) + BAND_LO
    phase = freq[:, None] * np.arange(lag_count, dtype=np.int64)[None, :] % lag_count
    angle = (2.0 * math.pi / lag_count * phase).astype(np.float32)
    scale = np.float32(1.0 / math.sqrt(bins))
    rows = [np.cos(angle) * scale, -np.sin(angle) * scale]
    return np.concatenate(rows, axis=0).astype(jnp.bfloat16)


def moves(n):
    every = range(n)
    return dict(
        chip=[(i, i ^ 1) for i in every],
        xs=[(i, i ^ 2) for i in every],
        xd=[(i, i ^ 3) for i in every],
        down=[(i, i - 4) for i in every if i >= 4],
        crossed=[(i, (i - 4) ^ 1) for i in every if i >= 4],
        up=[(i, i + 4) for i in every if i + 4 < n],
    )


def local(spectra, pair_offset, lag_limit):
    n = lax.axis_size("pairs")
    move = {name: functools.partial(lax.ppermute, axis_name="pairs", perm=perm) for name, perm in moves(n).items()}
    table = jnp.asarray(phase_table(spectra.shape[4], 2 * spectra.shape[4]))

    theirs, side_raw, up_raw, down_raw = quarters(spectra)
    got = move["chip"](theirs)
    down0 = move["down"](down_raw)
    side0 = move["xs"](side_raw)
    up0 = move["up"](up_raw)
    got_p, got_q, got_side = whiten_got(got)
    down1 = move["down"](got_p)
    side1 = move["xs"](got_side)
    up1 = move["up"](got_q)
    mine_p = whiten_block(down_raw)
    mine_q = whiten_block(up_raw)
    (pair,) = cross(chip_kernel, (2,), mine_p, got_p, mine_q, got_q)
    side0 = whiten_block(side0, after=pair)
    down0 = whiten_block(down0, after=side0)
    up0 = whiten_block(up0, after=down0)

    (zs,) = cross(back_kernel, (4,), mine_q, got_q, up0, side0, side1, after=up0)
    xs, xd = cross(near_kernel, (2, 2), mine_q, got_q, down0, down1, side0, side1, after=zs)
    (zd,) = cross(back_kernel, (4,), mine_q, got_q, up1, side0, side1, after=xd)
    own_here, own_chip = cross(
        own_kernel, (6, 6), mine_p, got_p, down0, down1, side0, side1, pair, after=zd
    )
    zs = move["down"](zs)
    xs = move["xs"](xs)
    xd = move["xd"](xd)
    own_chip = move["chip"](own_chip)
    zd = move["crossed"](zd)
    slots = (pair_offset, lag_limit)
    out = lag_products(0, (0, 1), LARGE, *slots, own_here, xs, zs, table, None)
    out = lag_products(1, (0,), LARGE, *slots, own_chip, xd, None, table, out)
    return lag_products(1, (1,), SMALL, *slots, own_chip, xd, zd, table, out)


def solution(mesh):
    in_specs = (
        P(("hours", "pairs"), None, None, None, None),
        P(("hours", "pairs"), None),
        P(("hours", "pairs"), None),
    )
    out_specs = P(("hours", "pairs"), None, None, None)
    return jax.shard_map(local, mesh=mesh, in_specs=in_specs, out_specs=out_specs, check_vma=False)
```

```python
import functools
import math

import jax
import jax.numpy as jnp
import numpy as np
from jax import lax
from jax.experimental import pallas as pl
from jax.experimental.pallas import tpu as pltpu
from jax.sharding import PartitionSpec as P

BAND_LO = 16
TILE = 16
LANES = 128
VMEM_LIMIT = 16 * 1024 * 1024
VMEM_ALL = 50 * 1024 * 1024
WHITEN_TILE = 16

SMALL = pl.CostEstimate(flops=1000, bytes_accessed=1000, transcendentals=0)
LARGE = pl.CostEstimate(flops=10_000_000_000, bytes_accessed=40_000_000, transcendentals=0)
OUT_SPACE = pl.ANY


def whiten_rows(read, write, windows, rows):
    def one_window(w, _):
        for row in range(0, rows, WHITEN_TILE):
            block = pl.ds(row, WHITEN_TILE)
            values = read(w, block).astype(jnp.float32)
            power = jnp.sum(jnp.sum(values * values, axis=0), axis=-1, keepdims=True)
            power = power / (values.shape[0] * values.shape[-1])
            write(w, block, (values * lax.rsqrt(power + 1e-06)).astype(jnp.bfloat16))
        return 0

    lax.fori_loop(0, windows, one_window, 0)


def place():
    index = lax.axis_index("pairs")
    return lax.rem(index, 2), lax.rem(lax.div(index, 2), 2)


def quarters_kernel(spectra, theirs, side, up, down, sent):
    rows = side.shape[2]
    core, x = place()
    copies = []
    for k, half, target in (
        (0, core, down),
        (1, core, up),
        (1 - x, core, side),
        (0, 1 - core, theirs.at[0]),
        (1, 1 - core, theirs.at[1]),
    ):
        base = pl.multiple_of((2 * k + half) * rows, rows)
        source = spectra.at[0, :, :, pl.ds(base, rows), :]
        copies.append(pltpu.make_async_copy(source, target, sent.at[len(copies)]))
    for copy in copies:
        copy.start()
    for copy in copies:
        copy.wait()


def quarters(spectra):
    parts, windows, channels, bins = spectra.shape[1:]
    shape = (parts, windows, channels // 4, bins)
    return pl.pallas_call(
        quarters_kernel,
        out_shape=[jax.ShapeDtypeStruct((2,) + shape, jnp.bfloat16)]
        + [jax.ShapeDtypeStruct(shape, jnp.bfloat16)] * 3,
        in_specs=[pl.BlockSpec(memory_space=pl.ANY)],
        out_specs=[pl.BlockSpec(memory_space=OUT_SPACE)] * 4,
        scratch_shapes=[pltpu.SemaphoreType.DMA((5,))],
        compiler_params=pltpu.CompilerParams(vmem_limit_bytes=VMEM_ALL),
        cost_estimate=SMALL,
        name="quarters",
    )(spectra)


def whiten_got_kernel(got, p_out, q_out, side_out):
    windows, rows = got.shape[2], got.shape[3]
    _, x = place()
    for k, target in ((0, p_out), (1, q_out)):

        def read(w, block):
            return got[k, :, w, block, :]

        def write(w, block, values):
            target[:, w, block, :] = values

        whiten_rows(read, write, windows, rows)

    @pl.when(x == 0)
    def _():
        side_out[...] = q_out[...]

    @pl.when(x == 1)
    def _():
        side_out[...] = p_out[...]


def whiten_got(got):
    vmem = pl.BlockSpec(memory_space=pltpu.VMEM)
    return pl.pallas_call(
        whiten_got_kernel,
        out_shape=[jax.ShapeDtypeStruct(got.shape[1:], jnp.bfloat16)] * 3,
        in_specs=[vmem],
        out_specs=[vmem] * 3,
        compiler_params=pltpu.CompilerParams(vmem_limit_bytes=VMEM_LIMIT),
        cost_estimate=SMALL,
        name="whiten_got",
    )(got)


def whiten_block_kernel(source, *rest):
    target = rest[-1]

    def read(w, block):
        return source[:, w, block, :]

    def write(w, block, values):
        target[:, w, block, :] = values

    whiten_rows(read, write, source.shape[1], source.shape[2])


def whiten_block(block, after=None):
    vmem = pl.BlockSpec(memory_space=pltpu.VMEM)
    extra = [] if after is None else [after]
    return pl.pallas_call(
        whiten_block_kernel,
        out_shape=jax.ShapeDtypeStruct(block.shape, jnp.bfloat16),
        in_specs=[vmem] + [pl.BlockSpec(memory_space=pl.ANY)] * len(extra),
        out_specs=vmem,
        compiler_params=pltpu.CompilerParams(vmem_limit_bytes=VMEM_LIMIT),
        cost_estimate=SMALL,
        name="whiten_block",
    )(block, *extra)


def products(first, second, stores, rows, bins, windows):
    def one_tile(step, _):
        row = pl.multiple_of(step * TILE, TILE)
        for lane in range(0, bins, LANES):
            reals = [[0.0] * len(second) for _ in first]
            imags = [[0.0] * len(second) for _ in first]
            for w in range(windows):
                a = [[f(part, w, row, lane) for part in range(2)] for f in first]
                b = [[f(part, w, row, lane) for part in range(2)] for f in second]
                for i, (ar, ai) in enumerate(a):
                    for j, (br, bi) in enumerate(b):
                        if not stores[i][j]:
                            continue
                        reals[i][j] = reals[i][j] + (ar * br + ai * bi)
                        imags[i][j] = imags[i][j] + (ar * bi - ai * br)
            for i in range(len(first)):
                for j in range(len(second)):
                    for ref, spot in stores[i][j]:
                        scale = 1.0 / windows
                        ref[spot, pl.ds(row, TILE), pl.ds(lane, LANES)] = (
                            reals[i][j] * scale
                        ).astype(jnp.bfloat16)
                        ref[spot, pl.ds(row, TILE), pl.ds(bins + lane, LANES)] = (
                            imags[i][j] * scale
                        ).astype(jnp.bfloat16)
        return 0

    lax.fori_loop(0, rows // TILE, one_tile, 0)


def reader(ref, *lead):
    def read(part, w, row, lane):
        index = lead + (part, w, pl.ds(row, TILE), pl.ds(lane, LANES))
        return ref[index].astype(jnp.float32)

    return read


def spots(core, ref, base):
    return [[(ref, base + core)], [(ref, base + 1 - core)]]


def chip_kernel(mine_p, got_p, mine_q, got_q, pair):
    windows, rows, bins = mine_q.shape[1:]
    core, _ = place()
    run = functools.partial(products, rows=rows, bins=bins, windows=windows)
    for spot, own in enumerate(((mine_p, got_p), (mine_q, got_q))):
        both = [[(pair, spot)]]

        @pl.when(core == 0)
        def _():
            run([reader(own[0])], [reader(own[1])], [both])

        @pl.when(core == 1)
        def _():
            run([reader(own[1])], [reader(own[0])], [both])


def back_kernel(mine_q, got_q, up, side0, side1, after, back):
    windows, rows, bins = mine_q.shape[1:]
    core, x = place()
    run = functools.partial(products, [reader(up)], rows=rows, bins=bins, windows=windows)
    run([reader(mine_q), reader(got_q)], [spots(core, back, 2)])

    @pl.when(x == 1)
    def _():
        run([reader(side0), reader(side1)], [spots(core, back, 0)])


def near_kernel(mine_q, got_q, down0, down1, side, after, near):
    windows, rows, bins = mine_q.shape[1:]
    core, x = place()
    stores = [spots(core, near, 0)]
    run = functools.partial(products, [reader(side)], rows=rows, bins=bins, windows=windows)

    @pl.when(x == 0)
    def _():
        run([reader(down0), reader(down1)], stores)

    @pl.when(x == 1)
    def _():
        run([reader(mine_q), reader(got_q)], stores)


def own_kernel(mine_p, got_p, down0, down1, side0, side1, pair, after, here, chip):
    here[4:6] = pair[...]
    chip[4:6] = pair[...]
    windows, rows, bins = mine_p.shape[1:]
    core, x = place()
    own = [reader(mine_p), reader(got_p)]
    run = functools.partial(products, own, rows=rows, bins=bins, windows=windows)
    run([reader(down0), reader(down1)], [spots(core, here, 2), spots(core, chip, 2)])

    @pl.when(x == 0)
    def _():
        run([reader(side0), reader(side1)], [spots(core, here, 0), spots(core, chip, 0)])


def cross(kernel, counts, *blocks, after=None):
    rows, bins = blocks[0].shape[2:]
    extra = [] if after is None else [after]
    vmem = pl.BlockSpec(memory_space=pltpu.VMEM)
    return pl.pallas_call(
        kernel,
        out_shape=[jax.ShapeDtypeStruct((n, rows, 2 * bins), jnp.bfloat16) for n in counts],
        in_specs=[vmem] * len(blocks) + [pl.BlockSpec(memory_space=pl.ANY)] * len(extra),
        out_specs=[vmem] * len(counts),
        compiler_params=pltpu.CompilerParams(vmem_limit_bytes=VMEM_LIMIT),
        cost_estimate=SMALL,
        name=kernel.__name__,
    )(*blocks, *extra)


def lag_kernel(flip, classes, offsets, limits, own, side, back, table, out, cand, chosen, lagged, sent):
    core, x = place()
    half = core if flip == 0 else 1 - core
    rows, lags = own.shape[1], table.shape[1]
    for spot, k in enumerate(classes):
        part = pl.ds(spot * rows, rows)
        cand[0, part, :] = own[4 + k]
        cand[3:5, part, :] = own[2:4] if k == 0 else back[2:4]

        @pl.when(x == 0)
        def _():
            cand[1:3, part, :] = own[0:2] if k == 0 else side[...]

        @pl.when(x == 1)
        def _():
            cand[1:3, part, :] = side[...] if k == 0 else back[0:2]

    lag = lax.broadcasted_iota(jnp.int32, (1, lags), 1)
    distance = jnp.minimum(lag, lags - lag)
    height = len(classes) * rows
    for slot in range(out.shape[1]):
        offset = offsets[0, slot]
        chosen[pl.ds(slot * height, height), :] = cand[jnp.clip(offset - 1 + core, 0, 4)]
    product = jnp.dot(chosen[...], table[...], preferred_element_type=jnp.float32)
    copies = []
    for slot in range(out.shape[1]):
        limit = jnp.where(offsets[0, slot] > 0, limits[0, slot], 0)
        kept = jnp.where(distance < limit, product[slot * height : (slot + 1) * height], 0.0)
        lagged[slot] = kept.astype(jnp.bfloat16)
        for spot, k in enumerate(classes):
            target = pl.multiple_of((2 * k + half) * rows, rows)
            copies.append(
                pltpu.make_async_copy(
                    lagged.at[slot, pl.ds(spot * rows, rows), :],
                    out.at[0, slot, pl.ds(target, rows), :],
                    sent.at[slot, spot],
                )
            )
            copies[-1].start()
    for copy in copies:
        copy.wait()


def lag_products(flip, classes, cost, offsets, limits, own, side, back, table, earlier):
    rows, width = own.shape[1:]
    slots, lags = offsets.shape[1], table.shape[1]
    vmem = pl.BlockSpec(memory_space=pltpu.VMEM)
    smem = pl.BlockSpec(memory_space=pltpu.SMEM)
    pieces = [own, side] + ([] if back is None else [back]) + [table]
    extra = [] if earlier is None else [earlier]

    def kernel(*refs):
        refs = list(refs)
        if earlier is not None:
            del refs[2 + len(pieces)]
        if back is None:
            refs.insert(4, None)
        lag_kernel(flip, classes, *refs)

    return pl.pallas_call(
        kernel,
        out_shape=jax.ShapeDtypeStruct((1, slots, 4 * rows, lags), jnp.bfloat16),
        in_specs=[smem] * 2
        + [vmem] * len(pieces)
        + [pl.BlockSpec(memory_space=pl.ANY)] * len(extra),
        out_specs=pl.BlockSpec(memory_space=pl.ANY),
        scratch_shapes=[
            pltpu.VMEM((5, len(classes) * rows, width), jnp.bfloat16),
            pltpu.VMEM((slots * len(classes) * rows, width), jnp.bfloat16),
            pltpu.VMEM((slots, len(classes) * rows, lags), jnp.bfloat16),
            pltpu.SemaphoreType.DMA((slots, len(classes))),
        ],
        input_output_aliases={2 + len(pieces): 0} if extra else {},
        compiler_params=pltpu.CompilerParams(vmem_limit_bytes=VMEM_LIMIT),
        cost_estimate=cost,
        name="lags",
    )(offsets, limits, *pieces, *extra)


def phase_table(bins, lag_count):
    freq = np.arange(bins, dtype=np.int64) + BAND_LO
    phase = freq[:, None] * np.arange(lag_count, dtype=np.int64)[None, :] % lag_count
    angle = (2.0 * math.pi / lag_count * phase).astype(np.float32)
    scale = np.float32(1.0 / math.sqrt(bins))
    rows = [np.cos(angle) * scale, -np.sin(angle) * scale]
    return np.concatenate(rows, axis=0).astype(jnp.bfloat16)


def moves(n):
    every = range(n)
    return dict(
        chip=[(i, i ^ 1) for i in every],
        xs=[(i, i ^ 2) for i in every],
        xd=[(i, i ^ 3) for i in every],
        down=[(i, i - 4) for i in every if i >= 4],
        crossed=[(i, (i - 4) ^ 1) for i in every if i >= 4],
        up=[(i, i + 4) for i in every if i + 4 < n],
    )


def local(spectra, pair_offset, lag_limit):
    n = lax.axis_size("pairs")
    move = {name: functools.partial(lax.ppermute, axis_name="pairs", perm=perm) for name, perm in moves(n).items()}
    table = jnp.asarray(phase_table(spectra.shape[4], 2 * spectra.shape[4]))

    theirs, side_raw, up_raw, down_raw = quarters(spectra)
    got = move["chip"](theirs)
    down0 = move["down"](down_raw)
    side0 = move["xs"](side_raw)
    up0 = move["up"](up_raw)
    got_p, got_q, got_side = whiten_got(got)
    down1 = move["down"](got_p)
    side1 = move["xs"](got_side)
    up1 = move["up"](got_q)
    mine_p = whiten_block(down_raw)
    mine_q = whiten_block(up_raw)
    (pair,) = cross(chip_kernel, (2,), mine_p, got_p, mine_q, got_q)
    side0 = whiten_block(side0, after=pair)
    down0 = whiten_block(down0, after=side0)
    up0 = whiten_block(up0, after=down0)

    (zs,) = cross(back_kernel, (4,), mine_q, got_q, up0, side0, side1, after=up0)
    (xs,) = cross(near_kernel, (2,), mine_q, got_q, down0, down1, side0, after=zs)
    (zd,) = cross(back_kernel, (4,), mine_q, got_q, up1, side0, side1, after=xs)
    (xd,) = cross(near_kernel, (2,), mine_q, got_q, down0, down1, side1, after=zd)
    own_here, own_chip = cross(
        own_kernel, (6, 6), mine_p, got_p, down0, down1, side0, side1, pair, after=xd
    )
    zs = move["down"](zs)
    xs = move["xs"](xs)
    xd = move["xd"](xd)
    own_chip = move["chip"](own_chip)
    zd = move["crossed"](zd)
    slots = (pair_offset, lag_limit)
    out = lag_products(0, (0, 1), LARGE, *slots, own_here, xs, zs, table, None)
    out = lag_products(1, (0,), LARGE, *slots, own_chip, xd, None, table, out)
    return lag_products(1, (1,), SMALL, *slots, own_chip, xd, zd, table, out)


def solution(mesh):
    in_specs = (
        P(("hours", "pairs"), None, None, None, None),
        P(("hours", "pairs"), None),
        P(("hours", "pairs"), None),
    )
    out_specs = P(("hours", "pairs"), None, None, None)
    return jax.shard_map(local, mesh=mesh, in_specs=in_specs, out_specs=out_specs, check_vma=False)
```

```python
import functools
import math

import jax
import jax.numpy as jnp
import numpy as np
from jax import lax
from jax.experimental import pallas as pl
from jax.experimental.pallas import tpu as pltpu
from jax.sharding import PartitionSpec as P

BAND_LO = 16
TILE = 16
LANES = 128
VMEM_LIMIT = 16 * 1024 * 1024
VMEM_ALL = 50 * 1024 * 1024
WHITEN_TILE = 16

SMALL = pl.CostEstimate(flops=1000, bytes_accessed=1000, transcendentals=0)
LARGE = pl.CostEstimate(flops=10_000_000_000, bytes_accessed=40_000_000, transcendentals=0)
OUT_SPACE = pl.ANY


def whiten_rows(read, write, windows, rows):
    def one_window(w, _):
        for row in range(0, rows, WHITEN_TILE):
            block = pl.ds(row, WHITEN_TILE)
            values = read(w, block).astype(jnp.float32)
            power = jnp.sum(jnp.sum(values * values, axis=0), axis=-1, keepdims=True)
            power = power / (values.shape[0] * values.shape[-1])
            write(w, block, (values * lax.rsqrt(power + 1e-06)).astype(jnp.bfloat16))
        return 0

    lax.fori_loop(0, windows, one_window, 0)


def place():
    index = lax.axis_index("pairs")
    return lax.rem(index, 2), lax.rem(lax.div(index, 2), 2)


def quarters_kernel(spectra, theirs, side, up, down, sent):
    rows = side.shape[2]
    core, x = place()
    copies = []
    for k, half, target in (
        (0, core, down),
        (1, core, up),
        (1 - x, core, side),
        (0, 1 - core, theirs.at[0]),
        (1, 1 - core, theirs.at[1]),
    ):
        base = pl.multiple_of((2 * k + half) * rows, rows)
        source = spectra.at[0, :, :, pl.ds(base, rows), :]
        copies.append(pltpu.make_async_copy(source, target, sent.at[len(copies)]))
    for copy in copies:
        copy.start()
    for copy in copies:
        copy.wait()


def quarters(spectra):
    parts, windows, channels, bins = spectra.shape[1:]
    shape = (parts, windows, channels // 4, bins)
    return pl.pallas_call(
        quarters_kernel,
        out_shape=[jax.ShapeDtypeStruct((2,) + shape, jnp.bfloat16)]
        + [jax.ShapeDtypeStruct(shape, jnp.bfloat16)] * 3,
        in_specs=[pl.BlockSpec(memory_space=pl.ANY)],
        out_specs=[pl.BlockSpec(memory_space=OUT_SPACE)] * 4,
        scratch_shapes=[pltpu.SemaphoreType.DMA((5,))],
        compiler_params=pltpu.CompilerParams(vmem_limit_bytes=VMEM_ALL),
        cost_estimate=SMALL,
        name="quarters",
    )(spectra)


def whiten_got_kernel(got, p_out, q_out, side_out):
    windows, rows = got.shape[2], got.shape[3]
    _, x = place()
    for k, target in ((0, p_out), (1, q_out)):

        def read(w, block):
            return got[k, :, w, block, :]

        def write(w, block, values):
            target[:, w, block, :] = values

        whiten_rows(read, write, windows, rows)

    @pl.when(x == 0)
    def _():
        side_out[...] = q_out[...]

    @pl.when(x == 1)
    def _():
        side_out[...] = p_out[...]


def whiten_got(got):
    vmem = pl.BlockSpec(memory_space=pltpu.VMEM)
    return pl.pallas_call(
        whiten_got_kernel,
        out_shape=[jax.ShapeDtypeStruct(got.shape[1:], jnp.bfloat16)] * 3,
        in_specs=[vmem],
        out_specs=[vmem] * 3,
        compiler_params=pltpu.CompilerParams(vmem_limit_bytes=VMEM_LIMIT),
        cost_estimate=SMALL,
        name="whiten_got",
    )(got)


def whiten_block_kernel(source, *rest):
    target = rest[-1]

    def read(w, block):
        return source[:, w, block, :]

    def write(w, block, values):
        target[:, w, block, :] = values

    whiten_rows(read, write, source.shape[1], source.shape[2])


def whiten_block(block, after=None):
    vmem = pl.BlockSpec(memory_space=pltpu.VMEM)
    extra = [] if after is None else [after]
    return pl.pallas_call(
        whiten_block_kernel,
        out_shape=jax.ShapeDtypeStruct(block.shape, jnp.bfloat16),
        in_specs=[vmem] + [pl.BlockSpec(memory_space=pl.ANY)] * len(extra),
        out_specs=vmem,
        compiler_params=pltpu.CompilerParams(vmem_limit_bytes=VMEM_LIMIT),
        cost_estimate=SMALL,
        name="whiten_block",
    )(block, *extra)


def products(first, second, stores, rows, bins, windows):
    def one_tile(step, _):
        row = pl.multiple_of(step * TILE, TILE)
        for lane in range(0, bins, LANES):
            reals = [[0.0] * len(second) for _ in first]
            imags = [[0.0] * len(second) for _ in first]
            for w in range(windows):
                a = [[f(part, w, row, lane) for part in range(2)] for f in first]
                b = [[f(part, w, row, lane) for part in range(2)] for f in second]
                for i, (ar, ai) in enumerate(a):
                    for j, (br, bi) in enumerate(b):
                        if not stores[i][j]:
                            continue
                        reals[i][j] = reals[i][j] + (ar * br + ai * bi)
                        imags[i][j] = imags[i][j] + (ar * bi - ai * br)
            for i in range(len(first)):
                for j in range(len(second)):
                    for ref, spot in stores[i][j]:
                        scale = 1.0 / windows
                        ref[spot, pl.ds(row, TILE), pl.ds(lane, LANES)] = (
                            reals[i][j] * scale
                        ).astype(jnp.bfloat16)
                        ref[spot, pl.ds(row, TILE), pl.ds(bins + lane, LANES)] = (
                            imags[i][j] * scale
                        ).astype(jnp.bfloat16)
        return 0

    lax.fori_loop(0, rows // TILE, one_tile, 0)


def reader(ref, *lead):
    def read(part, w, row, lane):
        index = lead + (part, w, pl.ds(row, TILE), pl.ds(lane, LANES))
        return ref[index].astype(jnp.float32)

    return read


def spots(core, ref, base):
    return [[(ref, base + core)], [(ref, base + 1 - core)]]


def chip_kernel(mine_p, got_p, mine_q, got_q, pair):
    windows, rows, bins = mine_q.shape[1:]
    core, _ = place()
    run = functools.partial(products, rows=rows, bins=bins, windows=windows)
    for spot, own in enumerate(((mine_p, got_p), (mine_q, got_q))):
        both = [[(pair, spot)]]

        @pl.when(core == 0)
        def _():
            run([reader(own[0])], [reader(own[1])], [both])

        @pl.when(core == 1)
        def _():
            run([reader(own[1])], [reader(own[0])], [both])


def back_kernel(mine_q, got_q, up, side0, side1, after, back):
    windows, rows, bins = mine_q.shape[1:]
    core, x = place()
    run = functools.partial(products, [reader(up)], rows=rows, bins=bins, windows=windows)
    run([reader(mine_q), reader(got_q)], [spots(core, back, 2)])

    @pl.when(x == 1)
    def _():
        run([reader(side0), reader(side1)], [spots(core, back, 0)])


def near_kernel(mine_q, got_q, down0, down1, side, after, near):
    windows, rows, bins = mine_q.shape[1:]
    core, x = place()
    stores = [spots(core, near, 0)]
    run = functools.partial(products, [reader(side)], rows=rows, bins=bins, windows=windows)

    @pl.when(x == 0)
    def _():
        run([reader(down0), reader(down1)], stores)

    @pl.when(x == 1)
    def _():
        run([reader(mine_q), reader(got_q)], stores)


def own_kernel(mine_p, got_p, down0, down1, side0, side1, pair, after, here, chip):
    here[4:6] = pair[...]
    chip[4:6] = pair[...]
    windows, rows, bins = mine_p.shape[1:]
    core, x = place()
    own = [reader(mine_p), reader(got_p)]
    run = functools.partial(products, own, rows=rows, bins=bins, windows=windows)
    run([reader(down0), reader(down1)], [spots(core, here, 2), spots(core, chip, 2)])

    @pl.when(x == 0)
    def _():
        run([reader(side0), reader(side1)], [spots(core, here, 0), spots(core, chip, 0)])


def cross(kernel, counts, *blocks, after=None):
    rows, bins = blocks[0].shape[2:]
    extra = [] if after is None else [after]
    vmem = pl.BlockSpec(memory_space=pltpu.VMEM)
    return pl.pallas_call(
        kernel,
        out_shape=[jax.ShapeDtypeStruct((n, rows, 2 * bins), jnp.bfloat16) for n in counts],
        in_specs=[vmem] * len(blocks) + [pl.BlockSpec(memory_space=pl.ANY)] * len(extra),
        out_specs=[vmem] * len(counts),
        compiler_params=pltpu.CompilerParams(vmem_limit_bytes=VMEM_LIMIT),
        cost_estimate=SMALL,
        name=kernel.__name__,
    )(*blocks, *extra)


def lag_rows(classes, offsets, limits, own, side, back, table, lagged, cand, chosen):
    core, x = place()
    rows, lags = own.shape[1], table.shape[1]
    for spot, k in enumerate(classes):
        part = pl.ds(spot * rows, rows)
        cand[0, part, :] = own[4 + k]
        cand[3:5, part, :] = own[2:4] if k == 0 else back[2:4]

        @pl.when(x == 0)
        def _():
            cand[1:3, part, :] = own[0:2] if k == 0 else side[...]

        @pl.when(x == 1)
        def _():
            cand[1:3, part, :] = side[...] if k == 0 else back[0:2]

    lag = lax.broadcasted_iota(jnp.int32, (1, lags), 1)
    distance = jnp.minimum(lag, lags - lag)
    height, slots = len(classes) * rows, lagged.shape[0]
    for slot in range(slots):
        offset = offsets[0, slot]
        chosen[pl.ds(slot * height, height), :] = cand[jnp.clip(offset - 1 + core, 0, 4)]
    product = jnp.dot(chosen[...], table[...], preferred_element_type=jnp.float32)
    for slot in range(slots):
        limit = jnp.where(offsets[0, slot] > 0, limits[0, slot], 0)
        kept = jnp.where(distance < limit, product[slot * height : (slot + 1) * height], 0.0)
        lagged[slot] = kept.astype(jnp.bfloat16)


def lag_part(classes, offsets, limits, *pieces, choose=False):
    rows, width = pieces[0].shape[1:]
    slots, lags = offsets.shape[1], pieces[-1].shape[1]
    height = len(classes) * rows
    vmem = pl.BlockSpec(memory_space=pltpu.VMEM)
    smem = pl.BlockSpec(memory_space=pltpu.SMEM)

    def kernel(*refs):
        refs = list(refs)
        if 1 not in classes:
            refs.insert(4, None)
        if choose:
            choice, kept = refs.pop(7), refs.pop(7)
            core, _ = place()
            row = lax.broadcasted_iota(jnp.int32, (rows, 6 * rows), 0)
            column = lax.broadcasted_iota(jnp.int32, (rows, 6 * rows), 1)
            lag = lax.broadcasted_iota(jnp.int32, (1, lags), 1)
            distance = jnp.minimum(lag, lags - lag)
            for slot in range(slots):
                offset = refs[0][0, slot]
                spot = jnp.clip(offset - 1 + core, 0, 4) * rows
                choice[pl.ds(slot * rows, rows), :] = jnp.where(column == row + spot, 1.0, 0.0).astype(
                    jnp.bfloat16
                )
                limit = jnp.where(offset > 0, refs[1][0, slot], 0)
                kept[pl.ds(slot, 1), :] = jnp.where(distance < limit, 1.0, 0.0)
        lag_rows(classes, *refs)

    out_shape = [jax.ShapeDtypeStruct((slots, height, lags), jnp.bfloat16)]
    if choose:
        out_shape.append(jax.ShapeDtypeStruct((slots * rows, 6 * rows), jnp.bfloat16))
        out_shape.append(jax.ShapeDtypeStruct((slots, lags), jnp.float32))
    return pl.pallas_call(
        kernel,
        out_shape=out_shape,
        in_specs=[smem] * 2 + [vmem] * len(pieces),
        out_specs=[vmem] * len(out_shape),
        scratch_shapes=[
            pltpu.VMEM((5, height, width), jnp.bfloat16),
            pltpu.VMEM((slots * height, width), jnp.bfloat16),
        ],
        compiler_params=pltpu.CompilerParams(vmem_limit_bytes=VMEM_LIMIT),
        cost_estimate=LARGE,
        name="lags",
    )(offsets, limits, *pieces)


def last_kernel(own, side, back, table, straight, crossed, choice, kept, out, lagged, cand, sent):
    core, x = place()
    slots, rows = lagged.shape[:2]
    copies = []

    def leave(source, k, half):
        target = pl.multiple_of((2 * k + half) * rows, rows)
        target = out.at[0, :, pl.ds(target, rows), :]
        copies.append(pltpu.make_async_copy(source, target, sent.at[len(copies)]))
        copies[-1].start()

    leave(straight.at[:, pl.ds(0, rows), :], 0, core)
    leave(straight.at[:, pl.ds(rows, rows), :], 1, core)
    leave(crossed, 0, 1 - core)
    cand[0] = own[5]
    cand[3:5] = back[2:4]
    cand[5] = jnp.zeros(cand.shape[1:], cand.dtype)

    @pl.when(x == 0)
    def _():
        cand[1:3] = side[...]

    @pl.when(x == 1)
    def _():
        cand[1:3] = back[0:2]

    spectrum = jnp.dot(
        choice[...], cand[...].reshape(6 * rows, -1), preferred_element_type=jnp.float32
    ).astype(jnp.bfloat16)
    product = jnp.dot(spectrum, table[...], preferred_element_type=jnp.float32)
    for slot in range(slots):
        keep = kept[pl.ds(slot, 1), :] > 0.0
        part = jnp.where(keep, product[slot * rows : (slot + 1) * rows], 0.0)
        lagged[slot] = part.astype(jnp.bfloat16)
    leave(lagged, 1, 1 - core)
    for copy in copies:
        copy.wait()


def last_part(*pieces):
    rows, width = pieces[0].shape[1:]
    slots, _, lags = pieces[4].shape
    vmem = pl.BlockSpec(memory_space=pltpu.VMEM)
    return pl.pallas_call(
        last_kernel,
        out_shape=jax.ShapeDtypeStruct((1, slots, 4 * rows, lags), jnp.bfloat16),
        in_specs=[vmem] * len(pieces),
        out_specs=pl.BlockSpec(memory_space=pl.ANY),
        scratch_shapes=[
            pltpu.VMEM((slots, rows, lags), jnp.bfloat16),
            pltpu.VMEM((6, rows, width), jnp.bfloat16),
            pltpu.SemaphoreType.DMA((4,)),
        ],
        compiler_params=pltpu.CompilerParams(vmem_limit_bytes=VMEM_LIMIT),
        cost_estimate=SMALL,
        name="last",
    )(*pieces)


def phase_table(bins, lag_count):
    freq = np.arange(bins, dtype=np.int64) + BAND_LO
    phase = freq[:, None] * np.arange(lag_count, dtype=np.int64)[None, :] % lag_count
    angle = (2.0 * math.pi / lag_count * phase).astype(np.float32)
    scale = np.float32(1.0 / math.sqrt(bins))
    rows = [np.cos(angle) * scale, -np.sin(angle) * scale]
    return np.concatenate(rows, axis=0).astype(jnp.bfloat16)


def moves(n):
    every = range(n)
    return dict(
        chip=[(i, i ^ 1) for i in every],
        xs=[(i, i ^ 2) for i in every],
        xd=[(i, i ^ 3) for i in every],
        down=[(i, i - 4) for i in every if i >= 4],
        crossed=[(i, (i - 4) ^ 1) for i in every if i >= 4],
        up=[(i, i + 4) for i in every if i + 4 < n],
    )


def local(spectra, pair_offset, lag_limit):
    n = lax.axis_size("pairs")
    move = {name: functools.partial(lax.ppermute, axis_name="pairs", perm=perm) for name, perm in moves(n).items()}
    table = jnp.asarray(phase_table(spectra.shape[4], 2 * spectra.shape[4]))

    theirs, side_raw, up_raw, down_raw = quarters(spectra)
    got = move["chip"](theirs)
    down0 = move["down"](down_raw)
    side0 = move["xs"](side_raw)
    up0 = move["up"](up_raw)
    got_p, got_q, got_side = whiten_got(got)
    down1 = move["down"](got_p)
    side1 = move["xs"](got_side)
    up1 = move["up"](got_q)
    mine_p = whiten_block(down_raw)
    mine_q = whiten_block(up_raw)
    (pair,) = cross(chip_kernel, (2,), mine_p, got_p, mine_q, got_q)
    side0 = whiten_block(side0, after=pair)
    down0 = whiten_block(down0, after=side0)
    up0 = whiten_block(up0, after=down0)

    (zs,) = cross(back_kernel, (4,), mine_q, got_q, up0, side0, side1, after=up0)
    (xs,) = cross(near_kernel, (2,), mine_q, got_q, down0, down1, side0, after=zs)
    (zd,) = cross(back_kernel, (4,), mine_q, got_q, up1, side0, side1, after=xs)
    (xd,) = cross(near_kernel, (2,), mine_q, got_q, down0, down1, side1, after=zd)
    own_here, own_chip = cross(
        own_kernel, (6, 6), mine_p, got_p, down0, down1, side0, side1, pair, after=xd
    )
    zs = move["down"](zs)
    xs = move["xs"](xs)
    zd = move["crossed"](zd)
    xd = move["xd"](xd)
    own_chip = move["chip"](own_chip)
    slots = (pair_offset, lag_limit)
    (straight,) = lag_part((0, 1), *slots, own_here, xs, zs, table)
    crossed, choice, kept = lag_part((0,), *slots, own_chip, xd, table, choose=True)
    return last_part(own_chip, xd, zd, table, straight, crossed, choice, kept)


def solution(mesh):
    in_specs = (
        P(("hours", "pairs"), None, None, None, None),
        P(("hours", "pairs"), None),
        P(("hours", "pairs"), None),
    )
    out_specs = P(("hours", "pairs"), None, None, None)
    return jax.shard_map(local, mesh=mesh, in_specs=in_specs, out_specs=out_specs, check_vma=False)
```

```python
import functools
import math

import jax
import jax.numpy as jnp
import numpy as np
from jax import lax
from jax.experimental import pallas as pl
from jax.experimental.pallas import tpu as pltpu
from jax.sharding import PartitionSpec as P

BAND_LO = 16
TILE = 16
LANES = 128
VMEM_LIMIT = 16 * 1024 * 1024
VMEM_ALL = 50 * 1024 * 1024
WHITEN_TILE = 16

SMALL = pl.CostEstimate(flops=1000, bytes_accessed=1000, transcendentals=0)
LARGE = pl.CostEstimate(flops=10_000_000_000, bytes_accessed=40_000_000, transcendentals=0)
OUT_SPACE = pl.ANY


def whiten_rows(read, write, windows, rows):
    def one_window(w, _):
        for row in range(0, rows, WHITEN_TILE):
            block = pl.ds(row, WHITEN_TILE)
            values = read(w, block).astype(jnp.float32)
            power = jnp.sum(jnp.sum(values * values, axis=0), axis=-1, keepdims=True)
            power = power / (values.shape[0] * values.shape[-1])
            write(w, block, (values * lax.rsqrt(power + 1e-06)).astype(jnp.bfloat16))
        return 0

    lax.fori_loop(0, windows, one_window, 0)


def place():
    index = lax.axis_index("pairs")
    return lax.rem(index, 2), lax.rem(lax.div(index, 2), 2)


def quarters_kernel(spectra, theirs, side, up, down, sent):
    rows = side.shape[2]
    core, x = place()
    copies = []
    for k, half, target in (
        (0, core, down),
        (1, core, up),
        (1 - x, core, side),
        (0, 1 - core, theirs.at[0]),
        (1, 1 - core, theirs.at[1]),
    ):
        base = pl.multiple_of((2 * k + half) * rows, rows)
        source = spectra.at[0, :, :, pl.ds(base, rows), :]
        copies.append(pltpu.make_async_copy(source, target, sent.at[len(copies)]))
    for copy in copies:
        copy.start()
    for copy in copies:
        copy.wait()


def quarters(spectra):
    parts, windows, channels, bins = spectra.shape[1:]
    shape = (parts, windows, channels // 4, bins)
    return pl.pallas_call(
        quarters_kernel,
        out_shape=[jax.ShapeDtypeStruct((2,) + shape, jnp.bfloat16)]
        + [jax.ShapeDtypeStruct(shape, jnp.bfloat16)] * 3,
        in_specs=[pl.BlockSpec(memory_space=pl.ANY)],
        out_specs=[pl.BlockSpec(memory_space=OUT_SPACE)] * 4,
        scratch_shapes=[pltpu.SemaphoreType.DMA((5,))],
        compiler_params=pltpu.CompilerParams(vmem_limit_bytes=VMEM_ALL),
        cost_estimate=SMALL,
        name="quarters",
    )(spectra)


def whiten_got_kernel(got, p_out, q_out, side_out):
    windows, rows = got.shape[2], got.shape[3]
    _, x = place()
    for k, target in ((0, p_out), (1, q_out)):

        def read(w, block):
            return got[k, :, w, block, :]

        def write(w, block, values):
            target[:, w, block, :] = values

        whiten_rows(read, write, windows, rows)

    @pl.when(x == 0)
    def _():
        side_out[...] = q_out[...]

    @pl.when(x == 1)
    def _():
        side_out[...] = p_out[...]


def whiten_got(got):
    vmem = pl.BlockSpec(memory_space=pltpu.VMEM)
    return pl.pallas_call(
        whiten_got_kernel,
        out_shape=[jax.ShapeDtypeStruct(got.shape[1:], jnp.bfloat16)] * 3,
        in_specs=[vmem],
        out_specs=[vmem] * 3,
        compiler_params=pltpu.CompilerParams(vmem_limit_bytes=VMEM_LIMIT),
        cost_estimate=SMALL,
        name="whiten_got",
    )(got)


def whiten_block_kernel(source, *rest):
    target = rest[-1]

    def read(w, block):
        return source[:, w, block, :]

    def write(w, block, values):
        target[:, w, block, :] = values

    whiten_rows(read, write, source.shape[1], source.shape[2])


def whiten_block(block, after=None):
    vmem = pl.BlockSpec(memory_space=pltpu.VMEM)
    extra = [] if after is None else [after]
    return pl.pallas_call(
        whiten_block_kernel,
        out_shape=jax.ShapeDtypeStruct(block.shape, jnp.bfloat16),
        in_specs=[vmem] + [pl.BlockSpec(memory_space=pl.ANY)] * len(extra),
        out_specs=vmem,
        compiler_params=pltpu.CompilerParams(vmem_limit_bytes=VMEM_LIMIT),
        cost_estimate=SMALL,
        name="whiten_block",
    )(block, *extra)


def products(first, second, stores, rows, bins, windows):
    def one_tile(step, _):
        row = pl.multiple_of(step * TILE, TILE)
        for lane in range(0, bins, LANES):
            reals = [[0.0] * len(second) for _ in first]
            imags = [[0.0] * len(second) for _ in first]
            for w in range(windows):
                a = [[f(part, w, row, lane) for part in range(2)] for f in first]
                b = [[f(part, w, row, lane) for part in range(2)] for f in second]
                for i, (ar, ai) in enumerate(a):
                    for j, (br, bi) in enumerate(b):
                        if not stores[i][j]:
                            continue
                        reals[i][j] = reals[i][j] + (ar * br + ai * bi)
                        imags[i][j] = imags[i][j] + (ar * bi - ai * br)
            for i in range(len(first)):
                for j in range(len(second)):
                    for ref, spot in stores[i][j]:
                        scale = 1.0 / windows
                        ref[spot, pl.ds(row, TILE), pl.ds(lane, LANES)] = (
                            reals[i][j] * scale
                        ).astype(jnp.bfloat16)
                        ref[spot, pl.ds(row, TILE), pl.ds(bins + lane, LANES)] = (
                            imags[i][j] * scale
                        ).astype(jnp.bfloat16)
        return 0

    lax.fori_loop(0, rows // TILE, one_tile, 0)


def reader(ref, *lead):
    def read(part, w, row, lane):
        index = lead + (part, w, pl.ds(row, TILE), pl.ds(lane, LANES))
        return ref[index].astype(jnp.float32)

    return read


def spots(core, ref, base):
    return [[(ref, base + core)], [(ref, base + 1 - core)]]


def chip_kernel(mine_p, got_p, mine_q, got_q, pair):
    windows, rows, bins = mine_q.shape[1:]
    core, _ = place()
    run = functools.partial(products, rows=rows, bins=bins, windows=windows)
    for spot, own in enumerate(((mine_p, got_p), (mine_q, got_q))):
        both = [[(pair, spot)]]

        @pl.when(core == 0)
        def _():
            run([reader(own[0])], [reader(own[1])], [both])

        @pl.when(core == 1)
        def _():
            run([reader(own[1])], [reader(own[0])], [both])


def early_kernel(mine_q, got_q, up0, side0, down0, after, far, near):
    windows, rows, bins = mine_q.shape[1:]
    core, x = place()
    run = functools.partial(products, rows=rows, bins=bins, windows=windows)
    own_q = [reader(mine_q), reader(got_q)]
    run([reader(up0)], own_q, [spots(core, far, 0)])

    @pl.when(x == 0)
    def _():
        run([reader(side0)], [reader(down0)], [spots(core, near, 0)[:1]])

    @pl.when(x == 1)
    def _():
        run([reader(side0)], own_q, [spots(core, near, 0)])


def back_straight_kernel(up, side0, side1, far, back):
    windows, rows, bins = up.shape[1:]
    core, x = place()
    back[2:4] = far[...]

    @pl.when(x == 1)
    def _():
        side = [reader(side0), reader(side1)]
        products([reader(up)], side, [spots(core, back, 0)], rows, bins, windows)


def near_straight_kernel(side, down1, early, after, near):
    windows, rows, bins = side.shape[1:]
    core, x = place()
    near[...] = early[...]

    @pl.when(x == 0)
    def _():
        stores = [spots(core, near, 0)[1:]]
        products([reader(side)], [reader(down1)], stores, rows, bins, windows)


def back_kernel(mine_q, got_q, up, side0, side1, after, back):
    windows, rows, bins = mine_q.shape[1:]
    core, x = place()
    run = functools.partial(products, [reader(up)], rows=rows, bins=bins, windows=windows)
    run([reader(mine_q), reader(got_q)], [spots(core, back, 2)])

    @pl.when(x == 1)
    def _():
        run([reader(side0), reader(side1)], [spots(core, back, 0)])


def near_kernel(mine_q, got_q, down0, down1, side, after, near):
    windows, rows, bins = mine_q.shape[1:]
    core, x = place()
    stores = [spots(core, near, 0)]
    run = functools.partial(products, [reader(side)], rows=rows, bins=bins, windows=windows)

    @pl.when(x == 0)
    def _():
        run([reader(down0), reader(down1)], stores)

    @pl.when(x == 1)
    def _():
        run([reader(mine_q), reader(got_q)], stores)


def own_kernel(mine_p, got_p, down0, down1, side0, side1, pair, after, here, chip):
    here[4:6] = pair[...]
    chip[4:6] = pair[...]
    windows, rows, bins = mine_p.shape[1:]
    core, x = place()
    own = [reader(mine_p), reader(got_p)]
    run = functools.partial(products, own, rows=rows, bins=bins, windows=windows)
    run([reader(down0), reader(down1)], [spots(core, here, 2), spots(core, chip, 2)])

    @pl.when(x == 0)
    def _():
        run([reader(side0), reader(side1)], [spots(core, here, 0), spots(core, chip, 0)])


def cross(kernel, counts, *blocks, after=None):
    rows, bins = blocks[0].shape[2:]
    extra = [] if after is None else [after]
    vmem = pl.BlockSpec(memory_space=pltpu.VMEM)
    return pl.pallas_call(
        kernel,
        out_shape=[jax.ShapeDtypeStruct((n, rows, 2 * bins), jnp.bfloat16) for n in counts],
        in_specs=[vmem] * len(blocks) + [pl.BlockSpec(memory_space=pl.ANY)] * len(extra),
        out_specs=[vmem] * len(counts),
        compiler_params=pltpu.CompilerParams(vmem_limit_bytes=VMEM_LIMIT),
        cost_estimate=SMALL,
        name=kernel.__name__,
    )(*blocks, *extra)


def lag_rows(classes, offsets, limits, own, side, back, table, lagged, cand, chosen):
    core, x = place()
    rows, lags = own.shape[1], table.shape[1]
    for spot, k in enumerate(classes):
        part = pl.ds(spot * rows, rows)
        cand[0, part, :] = own[4 + k]
        cand[3:5, part, :] = own[2:4] if k == 0 else back[2:4]

        @pl.when(x == 0)
        def _():
            cand[1:3, part, :] = own[0:2] if k == 0 else side[...]

        @pl.when(x == 1)
        def _():
            cand[1:3, part, :] = side[...] if k == 0 else back[0:2]

    lag = lax.broadcasted_iota(jnp.int32, (1, lags), 1)
    distance = jnp.minimum(lag, lags - lag)
    height, slots = len(classes) * rows, lagged.shape[0]
    for slot in range(slots):
        offset = offsets[0, slot]
        chosen[pl.ds(slot * height, height), :] = cand[jnp.clip(offset - 1 + core, 0, 4)]
    product = jnp.dot(chosen[...], table[...], preferred_element_type=jnp.float32)
    for slot in range(slots):
        limit = jnp.where(offsets[0, slot] > 0, limits[0, slot], 0)
        kept = jnp.where(distance < limit, product[slot * height : (slot + 1) * height], 0.0)
        lagged[slot] = kept.astype(jnp.bfloat16)


def lag_part(classes, offsets, limits, *pieces, choose=False):
    rows, width = pieces[0].shape[1:]
    slots, lags = offsets.shape[1], pieces[-1].shape[1]
    height = len(classes) * rows
    vmem = pl.BlockSpec(memory_space=pltpu.VMEM)
    smem = pl.BlockSpec(memory_space=pltpu.SMEM)

    def kernel(*refs):
        refs = list(refs)
        if 1 not in classes:
            refs.insert(4, None)
        if choose:
            choice, kept = refs.pop(7), refs.pop(7)
            core, _ = place()
            row = lax.broadcasted_iota(jnp.int32, (rows, 6 * rows), 0)
            column = lax.broadcasted_iota(jnp.int32, (rows, 6 * rows), 1)
            lag = lax.broadcasted_iota(jnp.int32, (1, lags), 1)
            distance = jnp.minimum(lag, lags - lag)
            for slot in range(slots):
                offset = refs[0][0, slot]
                spot = jnp.clip(offset - 1 + core, 0, 4) * rows
                choice[pl.ds(slot * rows, rows), :] = jnp.where(column == row + spot, 1.0, 0.0).astype(
                    jnp.bfloat16
                )
                limit = jnp.where(offset > 0, refs[1][0, slot], 0)
                kept[pl.ds(slot, 1), :] = jnp.where(distance < limit, 1.0, 0.0)
        lag_rows(classes, *refs)

    out_shape = [jax.ShapeDtypeStruct((slots, height, lags), jnp.bfloat16)]
    if choose:
        out_shape.append(jax.ShapeDtypeStruct((slots * rows, 6 * rows), jnp.bfloat16))
        out_shape.append(jax.ShapeDtypeStruct((slots, lags), jnp.float32))
    return pl.pallas_call(
        kernel,
        out_shape=out_shape,
        in_specs=[smem] * 2 + [vmem] * len(pieces),
        out_specs=[vmem] * len(out_shape),
        scratch_shapes=[
            pltpu.VMEM((5, height, width), jnp.bfloat16),
            pltpu.VMEM((slots * height, width), jnp.bfloat16),
        ],
        compiler_params=pltpu.CompilerParams(vmem_limit_bytes=VMEM_LIMIT),
        cost_estimate=LARGE,
        name="lags",
    )(offsets, limits, *pieces)


def last_kernel(own, side, back, table, straight, crossed, choice, kept, out, lagged, cand, sent):
    core, x = place()
    slots, rows = lagged.shape[:2]
    copies = []

    def leave(source, k, half):
        target = pl.multiple_of((2 * k + half) * rows, rows)
        target = out.at[0, :, pl.ds(target, rows), :]
        copies.append(pltpu.make_async_copy(source, target, sent.at[len(copies)]))
        copies[-1].start()

    leave(straight.at[:, pl.ds(0, rows), :], 0, core)
    leave(straight.at[:, pl.ds(rows, rows), :], 1, core)
    leave(crossed, 0, 1 - core)
    cand[0] = own[5]
    cand[3:5] = back[2:4]
    cand[5] = jnp.zeros(cand.shape[1:], cand.dtype)

    @pl.when(x == 0)
    def _():
        cand[1:3] = side[...]

    @pl.when(x == 1)
    def _():
        cand[1:3] = back[0:2]

    spectrum = jnp.dot(
        choice[...], cand[...].reshape(6 * rows, -1), preferred_element_type=jnp.float32
    ).astype(jnp.bfloat16)
    product = jnp.dot(spectrum, table[...], preferred_element_type=jnp.float32)
    for slot in range(slots):
        keep = kept[pl.ds(slot, 1), :] > 0.0
        part = jnp.where(keep, product[slot * rows : (slot + 1) * rows], 0.0)
        lagged[slot] = part.astype(jnp.bfloat16)
    leave(lagged, 1, 1 - core)
    for copy in copies:
        copy.wait()


def last_part(*pieces):
    rows, width = pieces[0].shape[1:]
    slots, _, lags = pieces[4].shape
    vmem = pl.BlockSpec(memory_space=pltpu.VMEM)
    return pl.pallas_call(
        last_kernel,
        out_shape=jax.ShapeDtypeStruct((1, slots, 4 * rows, lags), jnp.bfloat16),
        in_specs=[vmem] * len(pieces),
        out_specs=pl.BlockSpec(memory_space=pl.ANY),
        scratch_shapes=[
            pltpu.VMEM((slots, rows, lags), jnp.bfloat16),
            pltpu.VMEM((6, rows, width), jnp.bfloat16),
            pltpu.SemaphoreType.DMA((4,)),
        ],
        compiler_params=pltpu.CompilerParams(vmem_limit_bytes=VMEM_LIMIT),
        cost_estimate=SMALL,
        name="last",
    )(*pieces)


def phase_table(bins, lag_count):
    freq = np.arange(bins, dtype=np.int64) + BAND_LO
    phase = freq[:, None] * np.arange(lag_count, dtype=np.int64)[None, :] % lag_count
    angle = (2.0 * math.pi / lag_count * phase).astype(np.float32)
    scale = np.float32(1.0 / math.sqrt(bins))
    rows = [np.cos(angle) * scale, -np.sin(angle) * scale]
    return np.concatenate(rows, axis=0).astype(jnp.bfloat16)


def moves(n):
    every = range(n)
    return dict(
        chip=[(i, i ^ 1) for i in every],
        xs=[(i, i ^ 2) for i in every],
        xd=[(i, i ^ 3) for i in every],
        down=[(i, i - 4) for i in every if i >= 4],
        crossed=[(i, (i - 4) ^ 1) for i in every if i >= 4],
        up=[(i, i + 4) for i in every if i + 4 < n],
    )


def local(spectra, pair_offset, lag_limit):
    n = lax.axis_size("pairs")
    move = {name: functools.partial(lax.ppermute, axis_name="pairs", perm=perm) for name, perm in moves(n).items()}
    table = jnp.asarray(phase_table(spectra.shape[4], 2 * spectra.shape[4]))

    theirs, side_raw, up_raw, down_raw = quarters(spectra)
    got = move["chip"](theirs)
    down0 = move["down"](down_raw)
    side0 = move["xs"](side_raw)
    up0 = move["up"](up_raw)
    got_p, got_q, got_side = whiten_got(got)
    down1 = move["down"](got_p)
    side1 = move["xs"](got_side)
    up1 = move["up"](got_q)
    mine_p = whiten_block(down_raw)
    mine_q = whiten_block(up_raw)
    (pair,) = cross(chip_kernel, (2,), mine_p, got_p, mine_q, got_q)
    side0 = whiten_block(side0, after=pair)
    down0 = whiten_block(down0, after=side0)
    up0 = whiten_block(up0, after=down0)

    far, near = cross(early_kernel, (2, 2), mine_q, got_q, up0, side0, down0, after=up0)
    (zs,) = cross(back_straight_kernel, (4,), up0, side0, side1, far)
    (xs,) = cross(near_straight_kernel, (2,), side0, down1, near, after=zs)
    (zd,) = cross(back_kernel, (4,), mine_q, got_q, up1, side0, side1, after=xs)
    (xd,) = cross(near_kernel, (2,), mine_q, got_q, down0, down1, side1, after=zd)
    own_here, own_chip = cross(
        own_kernel, (6, 6), mine_p, got_p, down0, down1, side0, side1, pair, after=xd
    )
    zs = move["down"](zs)
    xs = move["xs"](xs)
    zd = move["crossed"](zd)
    xd = move["xd"](xd)
    own_chip = move["chip"](own_chip)
    slots = (pair_offset, lag_limit)
    (straight,) = lag_part((0, 1), *slots, own_here, xs, zs, table)
    crossed, choice, kept = lag_part((0,), *slots, own_chip, xd, table, choose=True)
    return last_part(own_chip, xd, zd, table, straight, crossed, choice, kept)


def solution(mesh):
    in_specs = (
        P(("hours", "pairs"), None, None, None, None),
        P(("hours", "pairs"), None),
        P(("hours", "pairs"), None),
    )
    out_specs = P(("hours", "pairs"), None, None, None)
    return jax.shard_map(local, mesh=mesh, in_specs=in_specs, out_specs=out_specs, check_vma=False)
```

```python
import functools
import math

import jax
import jax.numpy as jnp
import numpy as np
from jax import lax
from jax.experimental import pallas as pl
from jax.experimental.pallas import tpu as pltpu
from jax.sharding import PartitionSpec as P

BAND_LO = 16
TILE = 16
LANES = 128
VMEM_LIMIT = 16 * 1024 * 1024
VMEM_ALL = 51 * 1024 * 1024
WHITEN_TILE = 16

SMALL = pl.CostEstimate(flops=1000, bytes_accessed=1000, transcendentals=0)
LARGE = pl.CostEstimate(flops=10_000_000_000, bytes_accessed=40_000_000, transcendentals=0)
OUT_SPACE = pl.ANY


def whiten_rows(read, write, windows, rows):
    def one_window(w, _):
        for row in range(0, rows, WHITEN_TILE):
            block = pl.ds(row, WHITEN_TILE)
            values = read(w, block).astype(jnp.float32)
            power = jnp.sum(jnp.sum(values * values, axis=0), axis=-1, keepdims=True)
            power = power / (values.shape[0] * values.shape[-1])
            write(w, block, (values * lax.rsqrt(power + 1e-06)).astype(jnp.bfloat16))
        return 0

    lax.fori_loop(0, windows, one_window, 0)


def place():
    index = lax.axis_index("pairs")
    return lax.rem(index, 2), lax.rem(lax.div(index, 2), 2)


def quarters_kernel(spectra, side, up, down, sent):
    rows = side.shape[2]
    core, x = place()
    copies = []
    for k, half, target in (
        (0, core, down),
        (1, core, up),
        (1 - x, core, side),
    ):
        base = pl.multiple_of((2 * k + half) * rows, rows)
        source = spectra.at[0, :, :, pl.ds(base, rows), :]
        copies.append(pltpu.make_async_copy(source, target, sent.at[len(copies)]))
    for copy in copies:
        copy.start()
    for copy in copies:
        copy.wait()


def quarters(spectra):
    parts, windows, channels, bins = spectra.shape[1:]
    shape = (parts, windows, channels // 4, bins)
    return pl.pallas_call(
        quarters_kernel,
        out_shape=[jax.ShapeDtypeStruct(shape, jnp.bfloat16)] * 3,
        in_specs=[pl.BlockSpec(memory_space=pl.ANY)],
        out_specs=[pl.BlockSpec(memory_space=OUT_SPACE)] * 3,
        scratch_shapes=[pltpu.SemaphoreType.DMA((3,))],
        compiler_params=pltpu.CompilerParams(vmem_limit_bytes=VMEM_ALL),
        cost_estimate=SMALL,
        name="quarters",
    )(spectra)


def whiten_got_kernel(got, p_out, q_out, side_out):
    windows, rows = p_out.shape[1:3]
    core, x = place()
    for k, target in ((0, p_out), (1, q_out)):
        base = pl.multiple_of((2 * k + core) * rows, rows)

        def read(w, block):
            return got[0, :, w, pl.ds(base + block.start, block.size), :]

        def write(w, block, values):
            target[:, w, block, :] = values

        whiten_rows(read, write, windows, rows)

    @pl.when(x == 0)
    def _():
        side_out[...] = q_out[...]

    @pl.when(x == 1)
    def _():
        side_out[...] = p_out[...]


def whiten_got(got):
    parts, windows, channels, bins = got.shape[1:]
    shape = (parts, windows, channels // 4, bins)
    vmem = pl.BlockSpec(memory_space=pltpu.VMEM)
    return pl.pallas_call(
        whiten_got_kernel,
        out_shape=[jax.ShapeDtypeStruct(shape, jnp.bfloat16)] * 3,
        in_specs=[vmem],
        out_specs=[vmem] * 3,
        compiler_params=pltpu.CompilerParams(vmem_limit_bytes=VMEM_LIMIT),
        cost_estimate=SMALL,
        name="whiten_got",
    )(got)


def whiten_block_kernel(source, *rest):
    target = rest[-1]

    def read(w, block):
        return source[:, w, block, :]

    def write(w, block, values):
        target[:, w, block, :] = values

    whiten_rows(read, write, source.shape[1], source.shape[2])


def whiten_block(block, after=None):
    vmem = pl.BlockSpec(memory_space=pltpu.VMEM)
    extra = [] if after is None else [after]
    return pl.pallas_call(
        whiten_block_kernel,
        out_shape=jax.ShapeDtypeStruct(block.shape, jnp.bfloat16),
        in_specs=[vmem] + [pl.BlockSpec(memory_space=pl.ANY)] * len(extra),
        out_specs=vmem,
        compiler_params=pltpu.CompilerParams(vmem_limit_bytes=VMEM_LIMIT),
        cost_estimate=SMALL,
        name="whiten_block",
    )(block, *extra)


def products(first, second, stores, rows, bins, windows):
    def one_tile(step, _):
        row = pl.multiple_of(step * TILE, TILE)
        for lane in range(0, bins, LANES):
            reals = [[0.0] * len(second) for _ in first]
            imags = [[0.0] * len(second) for _ in first]
            for w in range(windows):
                a = [[f(part, w, row, lane) for part in range(2)] for f in first]
                b = [[f(part, w, row, lane) for part in range(2)] for f in second]
                for i, (ar, ai) in enumerate(a):
                    for j, (br, bi) in enumerate(b):
                        if not stores[i][j]:
                            continue
                        reals[i][j] = reals[i][j] + (ar * br + ai * bi)
                        imags[i][j] = imags[i][j] + (ar * bi - ai * br)
            for i in range(len(first)):
                for j in range(len(second)):
                    for ref, spot in stores[i][j]:
                        scale = 1.0 / windows
                        ref[spot, pl.ds(row, TILE), pl.ds(lane, LANES)] = (
                            reals[i][j] * scale
                        ).astype(jnp.bfloat16)
                        ref[spot, pl.ds(row, TILE), pl.ds(bins + lane, LANES)] = (
                            imags[i][j] * scale
                        ).astype(jnp.bfloat16)
        return 0

    lax.fori_loop(0, rows // TILE, one_tile, 0)


def reader(ref, *lead):
    def read(part, w, row, lane):
        index = lead + (part, w, pl.ds(row, TILE), pl.ds(lane, LANES))
        return ref[index].astype(jnp.float32)

    return read


def spots(core, ref, base):
    return [[(ref, base + core)], [(ref, base + 1 - core)]]


def chip_kernel(mine_p, got_p, mine_q, got_q, pair):
    windows, rows, bins = mine_q.shape[1:]
    core, _ = place()
    run = functools.partial(products, rows=rows, bins=bins, windows=windows)
    for spot, own in enumerate(((mine_p, got_p), (mine_q, got_q))):
        both = [[(pair, spot)]]

        @pl.when(core == 0)
        def _():
            run([reader(own[0])], [reader(own[1])], [both])

        @pl.when(core == 1)
        def _():
            run([reader(own[1])], [reader(own[0])], [both])


def early_kernel(mine_q, got_q, up0, side0, down0, after, far, near):
    windows, rows, bins = mine_q.shape[1:]
    core, x = place()
    run = functools.partial(products, rows=rows, bins=bins, windows=windows)
    own_q = [reader(mine_q), reader(got_q)]
    run([reader(up0)], own_q, [spots(core, far, 0)])

    @pl.when(x == 0)
    def _():
        run([reader(side0)], [reader(down0)], [spots(core, near, 0)[:1]])

    @pl.when(x == 1)
    def _():
        run([reader(side0)], own_q, [spots(core, near, 0)])


def back_straight_kernel(up, side0, side1, far, back):
    windows, rows, bins = up.shape[1:]
    core, x = place()
    back[2:4] = far[...]

    @pl.when(x == 1)
    def _():
        side = [reader(side0), reader(side1)]
        products([reader(up)], side, [spots(core, back, 0)], rows, bins, windows)


def near_straight_kernel(side, down1, early, after, near):
    windows, rows, bins = side.shape[1:]
    core, x = place()
    near[...] = early[...]

    @pl.when(x == 0)
    def _():
        stores = [spots(core, near, 0)[1:]]
        products([reader(side)], [reader(down1)], stores, rows, bins, windows)


def back_kernel(mine_q, got_q, up, side0, side1, after, back):
    windows, rows, bins = mine_q.shape[1:]
    core, x = place()
    run = functools.partial(products, [reader(up)], rows=rows, bins=bins, windows=windows)
    run([reader(mine_q), reader(got_q)], [spots(core, back, 2)])

    @pl.when(x == 1)
    def _():
        run([reader(side0), reader(side1)], [spots(core, back, 0)])


def near_kernel(mine_q, got_q, down0, down1, side, after, near):
    windows, rows, bins = mine_q.shape[1:]
    core, x = place()
    stores = [spots(core, near, 0)]
    run = functools.partial(products, [reader(side)], rows=rows, bins=bins, windows=windows)

    @pl.when(x == 0)
    def _():
        run([reader(down0), reader(down1)], stores)

    @pl.when(x == 1)
    def _():
        run([reader(mine_q), reader(got_q)], stores)


def own_kernel(mine_p, got_p, down0, down1, side0, side1, pair, after, here, chip):
    here[4:6] = pair[...]
    chip[4:6] = pair[...]
    windows, rows, bins = mine_p.shape[1:]
    core, x = place()
    own = [reader(mine_p), reader(got_p)]
    run = functools.partial(products, own, rows=rows, bins=bins, windows=windows)
    run([reader(down0), reader(down1)], [spots(core, here, 2), spots(core, chip, 2)])

    @pl.when(x == 0)
    def _():
        run([reader(side0), reader(side1)], [spots(core, here, 0), spots(core, chip, 0)])


def cross(kernel, counts, *blocks, after=None):
    rows, bins = blocks[0].shape[2:]
    extra = [] if after is None else [after]
    vmem = pl.BlockSpec(memory_space=pltpu.VMEM)
    return pl.pallas_call(
        kernel,
        out_shape=[jax.ShapeDtypeStruct((n, rows, 2 * bins), jnp.bfloat16) for n in counts],
        in_specs=[vmem] * len(blocks) + [pl.BlockSpec(memory_space=pl.ANY)] * len(extra),
        out_specs=[vmem] * len(counts),
        compiler_params=pltpu.CompilerParams(vmem_limit_bytes=VMEM_LIMIT),
        cost_estimate=SMALL,
        name=kernel.__name__,
    )(*blocks, *extra)


def lag_rows(classes, offsets, limits, own, side, back, table, lagged, cand, chosen):
    core, x = place()
    rows, lags = own.shape[1], table.shape[1]
    for spot, k in enumerate(classes):
        part = pl.ds(spot * rows, rows)
        cand[0, part, :] = own[4 + k]
        cand[3:5, part, :] = own[2:4] if k == 0 else back[2:4]

        @pl.when(x == 0)
        def _():
            cand[1:3, part, :] = own[0:2] if k == 0 else side[...]

        @pl.when(x == 1)
        def _():
            cand[1:3, part, :] = side[...] if k == 0 else back[0:2]

    lag = lax.broadcasted_iota(jnp.int32, (1, lags), 1)
    distance = jnp.minimum(lag, lags - lag)
    height, slots = len(classes) * rows, lagged.shape[0]
    for slot in range(slots):
        offset = offsets[0, slot]
        chosen[pl.ds(slot * height, height), :] = cand[jnp.clip(offset - 1 + core, 0, 4)]
    product = jnp.dot(chosen[...], table[...], preferred_element_type=jnp.float32)
    for slot in range(slots):
        limit = jnp.where(offsets[0, slot] > 0, limits[0, slot], 0)
        kept = jnp.where(distance < limit, product[slot * height : (slot + 1) * height], 0.0)
        lagged[slot] = kept.astype(jnp.bfloat16)


def lag_part(classes, offsets, limits, *pieces, choose=False):
    rows, width = pieces[0].shape[1:]
    slots, lags = offsets.shape[1], pieces[-1].shape[1]
    height = len(classes) * rows
    vmem = pl.BlockSpec(memory_space=pltpu.VMEM)
    smem = pl.BlockSpec(memory_space=pltpu.SMEM)

    def kernel(*refs):
        refs = list(refs)
        if 1 not in classes:
            refs.insert(4, None)
        if choose:
            choice, kept = refs.pop(7), refs.pop(7)
            core, _ = place()
            row = lax.broadcasted_iota(jnp.int32, (rows, 6 * rows), 0)
            column = lax.broadcasted_iota(jnp.int32, (rows, 6 * rows), 1)
            lag = lax.broadcasted_iota(jnp.int32, (1, lags), 1)
            distance = jnp.minimum(lag, lags - lag)
            for slot in range(slots):
                offset = refs[0][0, slot]
                spot = jnp.clip(offset - 1 + core, 0, 4) * rows
                choice[pl.ds(slot * rows, rows), :] = jnp.where(column == row + spot, 1.0, 0.0).astype(
                    jnp.bfloat16
                )
                limit = jnp.where(offset > 0, refs[1][0, slot], 0)
                kept[pl.ds(slot, 1), :] = jnp.where(distance < limit, 1.0, 0.0)
        lag_rows(classes, *refs)

    out_shape = [jax.ShapeDtypeStruct((slots, height, lags), jnp.bfloat16)]
    if choose:
        out_shape.append(jax.ShapeDtypeStruct((slots * rows, 6 * rows), jnp.bfloat16))
        out_shape.append(jax.ShapeDtypeStruct((slots, lags), jnp.float32))
    return pl.pallas_call(
        kernel,
        out_shape=out_shape,
        in_specs=[smem] * 2 + [vmem] * len(pieces),
        out_specs=[vmem] * len(out_shape),
        scratch_shapes=[
            pltpu.VMEM((5, height, width), jnp.bfloat16),
            pltpu.VMEM((slots * height, width), jnp.bfloat16),
        ],
        compiler_params=pltpu.CompilerParams(vmem_limit_bytes=VMEM_LIMIT),
        cost_estimate=LARGE,
        name="lags",
    )(offsets, limits, *pieces)


def last_kernel(own, side, back, table, straight, crossed, choice, kept, out, lagged, cand, sent):
    core, x = place()
    slots, rows = lagged.shape[:2]
    copies = []

    def leave(source, k, half):
        target = pl.multiple_of((2 * k + half) * rows, rows)
        target = out.at[0, :, pl.ds(target, rows), :]
        copies.append(pltpu.make_async_copy(source, target, sent.at[len(copies)]))
        copies[-1].start()

    leave(straight.at[:, pl.ds(0, rows), :], 0, core)
    leave(straight.at[:, pl.ds(rows, rows), :], 1, core)
    leave(crossed, 0, 1 - core)
    cand[0] = own[5]
    cand[3:5] = back[2:4]
    cand[5] = jnp.zeros(cand.shape[1:], cand.dtype)

    @pl.when(x == 0)
    def _():
        cand[1:3] = side[...]

    @pl.when(x == 1)
    def _():
        cand[1:3] = back[0:2]

    spectrum = jnp.dot(
        choice[...], cand[...].reshape(6 * rows, -1), preferred_element_type=jnp.float32
    ).astype(jnp.bfloat16)
    product = jnp.dot(spectrum, table[...], preferred_element_type=jnp.float32)
    for slot in range(slots):
        keep = kept[pl.ds(slot, 1), :] > 0.0
        part = jnp.where(keep, product[slot * rows : (slot + 1) * rows], 0.0)
        lagged[slot] = part.astype(jnp.bfloat16)
    leave(lagged, 1, 1 - core)
    for copy in copies:
        copy.wait()


def last_part(*pieces):
    rows, width = pieces[0].shape[1:]
    slots, _, lags = pieces[4].shape
    vmem = pl.BlockSpec(memory_space=pltpu.VMEM)
    return pl.pallas_call(
        last_kernel,
        out_shape=jax.ShapeDtypeStruct((1, slots, 4 * rows, lags), jnp.bfloat16),
        in_specs=[vmem] * len(pieces),
        out_specs=pl.BlockSpec(memory_space=pl.ANY),
        scratch_shapes=[
            pltpu.VMEM((slots, rows, lags), jnp.bfloat16),
            pltpu.VMEM((6, rows, width), jnp.bfloat16),
            pltpu.SemaphoreType.DMA((4,)),
        ],
        compiler_params=pltpu.CompilerParams(vmem_limit_bytes=VMEM_LIMIT),
        cost_estimate=SMALL,
        name="last",
    )(*pieces)


def phase_table(bins, lag_count):
    freq = np.arange(bins, dtype=np.int64) + BAND_LO
    phase = freq[:, None] * np.arange(lag_count, dtype=np.int64)[None, :] % lag_count
    angle = (2.0 * math.pi / lag_count * phase).astype(np.float32)
    scale = np.float32(1.0 / math.sqrt(bins))
    rows = [np.cos(angle) * scale, -np.sin(angle) * scale]
    return np.concatenate(rows, axis=0).astype(jnp.bfloat16)


def moves(n):
    every = range(n)
    return dict(
        chip=[(i, i ^ 1) for i in every],
        xs=[(i, i ^ 2) for i in every],
        xd=[(i, i ^ 3) for i in every],
        down=[(i, i - 4) for i in every if i >= 4],
        crossed=[(i, (i - 4) ^ 1) for i in every if i >= 4],
        up=[(i, i + 4) for i in every if i + 4 < n],
    )


def local(spectra, pair_offset, lag_limit):
    n = lax.axis_size("pairs")
    move = {name: functools.partial(lax.ppermute, axis_name="pairs", perm=perm) for name, perm in moves(n).items()}
    table = jnp.asarray(phase_table(spectra.shape[4], 2 * spectra.shape[4]))

    got = move["chip"](spectra)
    side_raw, up_raw, down_raw = quarters(spectra)
    down0 = move["down"](down_raw)
    side0 = move["xs"](side_raw)
    up0 = move["up"](up_raw)
    got_p, got_q, got_side = whiten_got(got)
    down1 = move["down"](got_p)
    side1 = move["xs"](got_side)
    up1 = move["up"](got_q)
    mine_p = whiten_block(down_raw)
    mine_q = whiten_block(up_raw)
    (pair,) = cross(chip_kernel, (2,), mine_p, got_p, mine_q, got_q)
    side0 = whiten_block(side0, after=pair)
    down0 = whiten_block(down0, after=side0)
    up0 = whiten_block(up0, after=down0)

    far, near = cross(early_kernel, (2, 2), mine_q, got_q, up0, side0, down0, after=up0)
    (zs,) = cross(back_straight_kernel, (4,), up0, side0, side1, far)
    (xs,) = cross(near_straight_kernel, (2,), side0, down1, near, after=zs)
    (zd,) = cross(back_kernel, (4,), mine_q, got_q, up1, side0, side1, after=xs)
    (xd,) = cross(near_kernel, (2,), mine_q, got_q, down0, down1, side1, after=zd)
    own_here, own_chip = cross(
        own_kernel, (6, 6), mine_p, got_p, down0, down1, side0, side1, pair, after=xd
    )
    zs = move["down"](zs)
    xs = move["xs"](xs)
    zd = move["crossed"](zd)
    xd = move["xd"](xd)
    own_chip = move["chip"](own_chip)
    slots = (pair_offset, lag_limit)
    (straight,) = lag_part((0, 1), *slots, own_here, xs, zs, table)
    crossed, choice, kept = lag_part((0,), *slots, own_chip, xd, table, choose=True)
    return last_part(own_chip, xd, zd, table, straight, crossed, choice, kept)


def solution(mesh):
    in_specs = (
        P(("hours", "pairs"), None, None, None, None),
        P(("hours", "pairs"), None),
        P(("hours", "pairs"), None),
    )
    out_specs = P(("hours", "pairs"), None, None, None)
    return jax.shard_map(local, mesh=mesh, in_specs=in_specs, out_specs=out_specs, check_vma=False)
```

```python
import functools
import math

import jax
import jax.numpy as jnp
import numpy as np
from jax import lax
from jax.experimental import pallas as pl
from jax.experimental.pallas import tpu as pltpu
from jax.sharding import PartitionSpec as P

BAND_LO = 16
TILE = 16
LANES = 128
VMEM_LIMIT = 16 * 1024 * 1024
VMEM_ALL = 51 * 1024 * 1024
WHITEN_TILE = 16

SMALL = pl.CostEstimate(flops=1000, bytes_accessed=1000, transcendentals=0)
LARGE = pl.CostEstimate(flops=10_000_000_000, bytes_accessed=40_000_000, transcendentals=0)
OUT_SPACE = pl.ANY


def whiten_rows(read, write, windows, rows):
    def one_window(w, _):
        for row in range(0, rows, WHITEN_TILE):
            block = pl.ds(row, WHITEN_TILE)
            values = read(w, block).astype(jnp.float32)
            power = jnp.sum(jnp.sum(values * values, axis=0), axis=-1, keepdims=True)
            power = power / (values.shape[0] * values.shape[-1])
            write(w, block, (values * lax.rsqrt(power + 1e-06)).astype(jnp.bfloat16))
        return 0

    lax.fori_loop(0, windows, one_window, 0, unroll=2)


def place():
    index = lax.axis_index("pairs")
    return lax.rem(index, 2), lax.rem(lax.div(index, 2), 2)


def quarters_kernel(spectra, side, up, down, sent):
    rows = side.shape[2]
    core, x = place()
    copies = []
    for k, half, target in (
        (0, core, down),
        (1, core, up),
        (1 - x, core, side),
    ):
        base = pl.multiple_of((2 * k + half) * rows, rows)
        source = spectra.at[0, :, :, pl.ds(base, rows), :]
        copies.append(pltpu.make_async_copy(source, target, sent.at[len(copies)]))
    for copy in copies:
        copy.start()
    for copy in copies:
        copy.wait()


def quarters(spectra):
    parts, windows, channels, bins = spectra.shape[1:]
    shape = (parts, windows, channels // 4, bins)
    return pl.pallas_call(
        quarters_kernel,
        out_shape=[jax.ShapeDtypeStruct(shape, jnp.bfloat16)] * 3,
        in_specs=[pl.BlockSpec(memory_space=pl.ANY)],
        out_specs=[pl.BlockSpec(memory_space=OUT_SPACE)] * 3,
        scratch_shapes=[pltpu.SemaphoreType.DMA((3,))],
        compiler_params=pltpu.CompilerParams(vmem_limit_bytes=VMEM_ALL),
        cost_estimate=SMALL,
        name="quarters",
    )(spectra)


def whiten_got_kernel(got, p_out, q_out, side_out):
    windows, rows = p_out.shape[1:3]
    core, x = place()
    for k, target in ((0, p_out), (1, q_out)):
        base = pl.multiple_of((2 * k + core) * rows, rows)

        def read(w, block):
            return got[0, :, w, pl.ds(base + block.start, block.size), :]

        def write(w, block, values):
            target[:, w, block, :] = values

        whiten_rows(read, write, windows, rows)

    @pl.when(x == 0)
    def _():
        side_out[...] = q_out[...]

    @pl.when(x == 1)
    def _():
        side_out[...] = p_out[...]


def whiten_got(got):
    parts, windows, channels, bins = got.shape[1:]
    shape = (parts, windows, channels // 4, bins)
    vmem = pl.BlockSpec(memory_space=pltpu.VMEM)
    return pl.pallas_call(
        whiten_got_kernel,
        out_shape=[jax.ShapeDtypeStruct(shape, jnp.bfloat16)] * 3,
        in_specs=[vmem],
        out_specs=[vmem] * 3,
        compiler_params=pltpu.CompilerParams(vmem_limit_bytes=VMEM_LIMIT),
        cost_estimate=SMALL,
        name="whiten_got",
    )(got)


def whiten_block_kernel(source, *rest):
    target = rest[-1]

    def read(w, block):
        return source[:, w, block, :]

    def write(w, block, values):
        target[:, w, block, :] = values

    whiten_rows(read, write, source.shape[1], source.shape[2])


def whiten_block(block, after=None):
    vmem = pl.BlockSpec(memory_space=pltpu.VMEM)
    extra = [] if after is None else [after]
    return pl.pallas_call(
        whiten_block_kernel,
        out_shape=jax.ShapeDtypeStruct(block.shape, jnp.bfloat16),
        in_specs=[vmem] + [pl.BlockSpec(memory_space=pl.ANY)] * len(extra),
        out_specs=vmem,
        compiler_params=pltpu.CompilerParams(vmem_limit_bytes=VMEM_LIMIT),
        cost_estimate=SMALL,
        name="whiten_block",
    )(block, *extra)


def products(first, second, stores, rows, bins, windows):
    def one_tile(step, _):
        row = pl.multiple_of(step * TILE, TILE)
        for lane in range(0, bins, LANES):
            reals = [[0.0] * len(second) for _ in first]
            imags = [[0.0] * len(second) for _ in first]
            for w in range(windows):
                a = [[f(part, w, row, lane) for part in range(2)] for f in first]
                b = [[f(part, w, row, lane) for part in range(2)] for f in second]
                for i, (ar, ai) in enumerate(a):
                    for j, (br, bi) in enumerate(b):
                        if not stores[i][j]:
                            continue
                        reals[i][j] = reals[i][j] + (ar * br + ai * bi)
                        imags[i][j] = imags[i][j] + (ar * bi - ai * br)
            for i in range(len(first)):
                for j in range(len(second)):
                    for ref, spot in stores[i][j]:
                        scale = 1.0 / windows
                        ref[spot, pl.ds(row, TILE), pl.ds(lane, LANES)] = (
                            reals[i][j] * scale
                        ).astype(jnp.bfloat16)
                        ref[spot, pl.ds(row, TILE), pl.ds(bins + lane, LANES)] = (
                            imags[i][j] * scale
                        ).astype(jnp.bfloat16)
        return 0

    lax.fori_loop(0, rows // TILE, one_tile, 0, unroll=4)


def reader(ref, *lead):
    def read(part, w, row, lane):
        index = lead + (part, w, pl.ds(row, TILE), pl.ds(lane, LANES))
        return ref[index].astype(jnp.float32)

    return read


def spots(core, ref, base):
    return [[(ref, base + core)], [(ref, base + 1 - core)]]


def chip_kernel(mine_p, got_p, mine_q, got_q, pair):
    windows, rows, bins = mine_q.shape[1:]
    core, _ = place()
    run = functools.partial(products, rows=rows, bins=bins, windows=windows)
    for spot, own in enumerate(((mine_p, got_p), (mine_q, got_q))):
        both = [[(pair, spot)]]

        @pl.when(core == 0)
        def _():
            run([reader(own[0])], [reader(own[1])], [both])

        @pl.when(core == 1)
        def _():
            run([reader(own[1])], [reader(own[0])], [both])


def early_kernel(mine_q, got_q, up0, side0, down0, after, far, near):
    windows, rows, bins = mine_q.shape[1:]
    core, x = place()
    run = functools.partial(products, rows=rows, bins=bins, windows=windows)
    own_q = [reader(mine_q), reader(got_q)]
    run([reader(up0)], own_q, [spots(core, far, 0)])

    @pl.when(x == 0)
    def _():
        run([reader(side0)], [reader(down0)], [spots(core, near, 0)[:1]])

    @pl.when(x == 1)
    def _():
        run([reader(side0)], own_q, [spots(core, near, 0)])


def back_straight_kernel(up, side0, side1, far, back):
    windows, rows, bins = up.shape[1:]
    core, x = place()
    back[2:4] = far[...]

    @pl.when(x == 1)
    def _():
        side = [reader(side0), reader(side1)]
        products([reader(up)], side, [spots(core, back, 0)], rows, bins, windows)


def near_straight_kernel(side, down1, early, after, near):
    windows, rows, bins = side.shape[1:]
    core, x = place()
    near[...] = early[...]

    @pl.when(x == 0)
    def _():
        stores = [spots(core, near, 0)[1:]]
        products([reader(side)], [reader(down1)], stores, rows, bins, windows)


def back_kernel(mine_q, got_q, up, side0, side1, after, back):
    windows, rows, bins = mine_q.shape[1:]
    core, x = place()
    run = functools.partial(products, [reader(up)], rows=rows, bins=bins, windows=windows)
    run([reader(mine_q), reader(got_q)], [spots(core, back, 2)])

    @pl.when(x == 1)
    def _():
        run([reader(side0), reader(side1)], [spots(core, back, 0)])


def near_kernel(mine_q, got_q, down0, down1, side, after, near):
    windows, rows, bins = mine_q.shape[1:]
    core, x = place()
    stores = [spots(core, near, 0)]
    run = functools.partial(products, [reader(side)], rows=rows, bins=bins, windows=windows)

    @pl.when(x == 0)
    def _():
        run([reader(down0), reader(down1)], stores)

    @pl.when(x == 1)
    def _():
        run([reader(mine_q), reader(got_q)], stores)


def own_kernel(mine_p, got_p, down0, down1, side0, side1, pair, after, here, chip):
    here[4:6] = pair[...]
    chip[4:6] = pair[...]
    windows, rows, bins = mine_p.shape[1:]
    core, x = place()
    own = [reader(mine_p), reader(got_p)]
    run = functools.partial(products, own, rows=rows, bins=bins, windows=windows)
    run([reader(down0), reader(down1)], [spots(core, here, 2), spots(core, chip, 2)])

    @pl.when(x == 0)
    def _():
        run([reader(side0), reader(side1)], [spots(core, here, 0), spots(core, chip, 0)])


def cross(kernel, counts, *blocks, after=None):
    rows, bins = blocks[0].shape[2:]
    extra = [] if after is None else [after]
    vmem = pl.BlockSpec(memory_space=pltpu.VMEM)
    return pl.pallas_call(
        kernel,
        out_shape=[jax.ShapeDtypeStruct((n, rows, 2 * bins), jnp.bfloat16) for n in counts],
        in_specs=[vmem] * len(blocks) + [pl.BlockSpec(memory_space=pl.ANY)] * len(extra),
        out_specs=[vmem] * len(counts),
        compiler_params=pltpu.CompilerParams(vmem_limit_bytes=VMEM_LIMIT),
        cost_estimate=SMALL,
        name=kernel.__name__,
    )(*blocks, *extra)


def lag_rows(classes, offsets, limits, own, side, back, table, lagged, cand, chosen):
    core, x = place()
    rows, lags = own.shape[1], table.shape[1]
    for spot, k in enumerate(classes):
        part = pl.ds(spot * rows, rows)
        cand[0, part, :] = own[4 + k]
        cand[3:5, part, :] = own[2:4] if k == 0 else back[2:4]

        @pl.when(x == 0)
        def _():
            cand[1:3, part, :] = own[0:2] if k == 0 else side[...]

        @pl.when(x == 1)
        def _():
            cand[1:3, part, :] = side[...] if k == 0 else back[0:2]

    lag = lax.broadcasted_iota(jnp.int32, (1, lags), 1)
    distance = jnp.minimum(lag, lags - lag)
    height, slots = len(classes) * rows, lagged.shape[0]
    for slot in range(slots):
        offset = offsets[0, slot]
        chosen[pl.ds(slot * height, height), :] = cand[jnp.clip(offset - 1 + core, 0, 4)]
    product = jnp.dot(chosen[...], table[...], preferred_element_type=jnp.float32)
    for slot in range(slots):
        limit = jnp.where(offsets[0, slot] > 0, limits[0, slot], 0)
        kept = jnp.where(distance < limit, product[slot * height : (slot + 1) * height], 0.0)
        lagged[slot] = kept.astype(jnp.bfloat16)


def lag_part(classes, offsets, limits, *pieces, choose=False):
    rows, width = pieces[0].shape[1:]
    slots, lags = offsets.shape[1], pieces[-1].shape[1]
    height = len(classes) * rows
    vmem = pl.BlockSpec(memory_space=pltpu.VMEM)
    smem = pl.BlockSpec(memory_space=pltpu.SMEM)

    def kernel(*refs):
        refs = list(refs)
        if 1 not in classes:
            refs.insert(4, None)
        if choose:
            choice, kept = refs.pop(7), refs.pop(7)
            core, _ = place()
            row = lax.broadcasted_iota(jnp.int32, (rows, 6 * rows), 0)
            column = lax.broadcasted_iota(jnp.int32, (rows, 6 * rows), 1)
            lag = lax.broadcasted_iota(jnp.int32, (1, lags), 1)
            distance = jnp.minimum(lag, lags - lag)
            for slot in range(slots):
                offset = refs[0][0, slot]
                spot = jnp.clip(offset - 1 + core, 0, 4) * rows
                choice[pl.ds(slot * rows, rows), :] = jnp.where(column == row + spot, 1.0, 0.0).astype(
                    jnp.bfloat16
                )
                limit = jnp.where(offset > 0, refs[1][0, slot], 0)
                kept[pl.ds(slot, 1), :] = jnp.where(distance < limit, 1.0, 0.0)
        lag_rows(classes, *refs)

    out_shape = [jax.ShapeDtypeStruct((slots, height, lags), jnp.bfloat16)]
    if choose:
        out_shape.append(jax.ShapeDtypeStruct((slots * rows, 6 * rows), jnp.bfloat16))
        out_shape.append(jax.ShapeDtypeStruct((slots, lags), jnp.float32))
    return pl.pallas_call(
        kernel,
        out_shape=out_shape,
        in_specs=[smem] * 2 + [vmem] * len(pieces),
        out_specs=[vmem] * len(out_shape),
        scratch_shapes=[
            pltpu.VMEM((5, height, width), jnp.bfloat16),
            pltpu.VMEM((slots * height, width), jnp.bfloat16),
        ],
        compiler_params=pltpu.CompilerParams(vmem_limit_bytes=VMEM_LIMIT),
        cost_estimate=LARGE,
        name="lags",
    )(offsets, limits, *pieces)


def last_kernel(own, side, back, table, straight, crossed, choice, kept, out, lagged, cand, sent):
    core, x = place()
    slots, rows = lagged.shape[:2]
    copies = []

    def leave(source, k, half, slot=slice(None)):
        target = pl.multiple_of((2 * k + half) * rows, rows)
        target = out.at[0, slot, pl.ds(target, rows), :]
        copies.append(pltpu.make_async_copy(source, target, sent.at[len(copies)]))
        copies[-1].start()

    leave(straight.at[:, pl.ds(0, rows), :], 0, core)
    leave(straight.at[:, pl.ds(rows, rows), :], 1, core)
    leave(crossed, 0, 1 - core)
    cand[0] = own[5]
    cand[3:5] = back[2:4]
    cand[5] = jnp.zeros(cand.shape[1:], cand.dtype)

    @pl.when(x == 0)
    def _():
        cand[1:3] = side[...]

    @pl.when(x == 1)
    def _():
        cand[1:3] = back[0:2]

    spectrum = jnp.dot(
        choice[...], cand[...].reshape(6 * rows, -1), preferred_element_type=jnp.float32
    ).astype(jnp.bfloat16)
    for slot in range(0, slots, 2):
        pair = spectrum[slot * rows : (slot + 2) * rows]
        product = jnp.dot(pair, table[...], preferred_element_type=jnp.float32)
        for near in range(2):
            keep = kept[pl.ds(slot + near, 1), :] > 0.0
            part = jnp.where(keep, product[near * rows : (near + 1) * rows], 0.0)
            lagged[slot + near] = part.astype(jnp.bfloat16)
            leave(lagged.at[slot + near], 1, 1 - core, slot + near)
    for copy in copies:
        copy.wait()


def last_part(*pieces):
    rows, width = pieces[0].shape[1:]
    slots, _, lags = pieces[4].shape
    vmem = pl.BlockSpec(memory_space=pltpu.VMEM)
    return pl.pallas_call(
        last_kernel,
        out_shape=jax.ShapeDtypeStruct((1, slots, 4 * rows, lags), jnp.bfloat16),
        in_specs=[vmem] * len(pieces),
        out_specs=pl.BlockSpec(memory_space=pl.ANY),
        scratch_shapes=[
            pltpu.VMEM((slots, rows, lags), jnp.bfloat16),
            pltpu.VMEM((6, rows, width), jnp.bfloat16),
            pltpu.SemaphoreType.DMA((3 + slots,)),
        ],
        compiler_params=pltpu.CompilerParams(vmem_limit_bytes=VMEM_LIMIT),
        cost_estimate=SMALL,
        name="last",
    )(*pieces)


def phase_table(bins, lag_count):
    freq = np.arange(bins, dtype=np.int64) + BAND_LO
    phase = freq[:, None] * np.arange(lag_count, dtype=np.int64)[None, :] % lag_count
    angle = (2.0 * math.pi / lag_count * phase).astype(np.float32)
    scale = np.float32(1.0 / math.sqrt(bins))
    rows = [np.cos(angle) * scale, -np.sin(angle) * scale]
    return np.concatenate(rows, axis=0).astype(jnp.bfloat16)


def moves(n):
    every = range(n)
    return dict(
        chip=[(i, i ^ 1) for i in every],
        xs=[(i, i ^ 2) for i in every],
        xd=[(i, i ^ 3) for i in every],
        down=[(i, i - 4) for i in every if i >= 4],
        crossed=[(i, (i - 4) ^ 1) for i in every if i >= 4],
        up=[(i, i + 4) for i in every if i + 4 < n],
    )


def local(spectra, pair_offset, lag_limit):
    n = lax.axis_size("pairs")
    move = {name: functools.partial(lax.ppermute, axis_name="pairs", perm=perm) for name, perm in moves(n).items()}
    table = jnp.asarray(phase_table(spectra.shape[4], 2 * spectra.shape[4]))

    got = move["chip"](spectra)
    side_raw, up_raw, down_raw = quarters(spectra)
    down0 = move["down"](down_raw)
    side0 = move["xs"](side_raw)
    up0 = move["up"](up_raw)
    got_p, got_q, got_side = whiten_got(got)
    down1 = move["down"](got_p)
    side1 = move["xs"](got_side)
    up1 = move["up"](got_q)
    mine_p = whiten_block(down_raw)
    mine_q = whiten_block(up_raw)
    (pair,) = cross(chip_kernel, (2,), mine_p, got_p, mine_q, got_q)
    side0 = whiten_block(side0, after=pair)
    down0 = whiten_block(down0, after=side0)
    up0 = whiten_block(up0, after=down0)

    far, near = cross(early_kernel, (2, 2), mine_q, got_q, up0, side0, down0, after=up0)
    (zs,) = cross(back_straight_kernel, (4,), up0, side0, side1, far)
    (xs,) = cross(near_straight_kernel, (2,), side0, down1, near, after=zs)
    (zd,) = cross(back_kernel, (4,), mine_q, got_q, up1, side0, side1, after=xs)
    (xd,) = cross(near_kernel, (2,), mine_q, got_q, down0, down1, side1, after=zd)
    own_here, own_chip = cross(
        own_kernel, (6, 6), mine_p, got_p, down0, down1, side0, side1, pair, after=xd
    )
    zs = move["down"](zs)
    xs = move["xs"](xs)
    zd = move["crossed"](zd)
    xd = move["xd"](xd)
    own_chip = move["chip"](own_chip)
    slots = (pair_offset, lag_limit)
    (straight,) = lag_part((0, 1), *slots, own_here, xs, zs, table)
    crossed, choice, kept = lag_part((0,), *slots, own_chip, xd, table, choose=True)
    return last_part(own_chip, xd, zd, table, straight, crossed, choice, kept)


def solution(mesh):
    in_specs = (
        P(("hours", "pairs"), None, None, None, None),
        P(("hours", "pairs"), None),
        P(("hours", "pairs"), None),
    )
    out_specs = P(("hours", "pairs"), None, None, None)
    return jax.shard_map(local, mesh=mesh, in_specs=in_specs, out_specs=out_specs, check_vma=False)
```
